512 devices in a mesh: gx: 4 (over y), gy: 8 (over x, core), gz: 16 (over z).
Axes of the slice: x: 4, y: 4, z: 16, core: 2. Of those that a mesh axis runs over, the one named last changes fastest.
Arguments:
- resid: bfloat16 [2, 64, 18432], P(None, None, ('gx', 'gy', 'gz')), may hold values from -6 to 6
- query: bfloat16 [2, 64, 12288], P(None, None, 'gz'), may hold values from -6 to 6
- new_kv: bfloat16 [2, 64, 512], P(None, 'gz'), may hold values from -6 to 6
- key_cache: bfloat16 [64, 4096, 256], P('gz', ('gx', 'gy')), may hold values from -4 to 4
- value_cache: bfloat16 [64, 4096, 256], P('gz', ('gx', 'gy')), may hold values from -6 to 6
- lengths: int32 [64], P('gz'), may hold values from 1024 to 4096, as said below
- out_weight: bfloat16 [12288, 18432], P(('gy', 'gz'), 'gx'), may hold values from -0.21875 to 0.21875
- hidden: bfloat16 [2, 64, 36864], P(None, 'gx', ('gy', 'gz')), may hold values from -6 to 6
- down_weight: bfloat16 [36864, 18432], P(('gy', 'gz'), 'gx'), may hold values from -0.125 to 0.125
Outputs:
- layer_out: bfloat16 [2, 64, 18432], P(None, None, ('gx', 'gy', 'gz'))
The draws below stay inside these ranges and needn't reach their ends.
Inputs may be any that keep to these rules, and one draw needn't show every extreme that they name: Transcript b attends to cache positions below lengths[b]; some transcript's length is 4096 in every draw.
All inputs are finite; a program needn't handle non-finite values.
Results may differ from the reference program's by a relative error of at most 0.0034.
Values may be sent and summed in bfloat16 or wider, within the bound.
No kernel may reach another device: no remote copies, remote signals or barrier semaphores. Data moves between devices by JAX's collectives and lax.ppermute only.
A program may use at most 64 MiB of HBM per device.

```python
import jax
import jax.numpy as jnp
from jax import lax

D = 18432
HEADS = 48
HD = 256
FW = 36864
B = 64
SEQ = 4096


def draw_query(key, part):
    base = jnp.clip(2.0 * jax.random.normal(key, (2, B, HEADS, HD), jnp.float32), -6.0, 6.0)
    return base.reshape(2, B, HEADS * HD).astype(jnp.bfloat16)


def draw_key_cache(key, part):
    base = jnp.clip(jax.random.normal(key, (B, SEQ, HD), jnp.float32), -4.0, 4.0)
    return base.astype(jnp.bfloat16)


def draw_lengths(key, part):
    first_key, second_key = jax.random.split(jax.random.fold_in(key, 11))
    values = jax.random.randint(first_key, (B,), SEQ // 4, SEQ + 1)
    longest = jax.random.randint(second_key, (), 0, B)
    return jnp.where(jnp.arange(B) == longest, SEQ, values).astype(jnp.int32)


def raised(array, rng, source, target, blocks, factor):
    owner, partner = [(jnp.arange(array.shape[position]) // (array.shape[position] // blocks)).reshape([-1 if axis == position else 1 for axis in range(array.ndim)]) for position in (source, target)]
    chosen = jax.random.permutation(rng, blocks)[partner]
    strong = (owner == chosen) | (owner == (partner + blocks // 2) % blocks)
    return jnp.where(strong, factor * array, array)


def shard_levels(stream_key, extent, shards, least, largest):
    level = 1.0
    for axis_at, blocks in shards:
        steps = jax.random.uniform(jax.random.fold_in(jax.random.fold_in(stream_key, 6), axis_at), (blocks,), jnp.float32, least / len(shards), largest / len(shards))
        level = level * jnp.repeat(jnp.exp(steps), extent[axis_at] // blocks).reshape((-1,) + (1,) * (len(extent) - 1 - axis_at))
    return level


def normal_values(stream_key, shape, width, bound, cuts=(), kind=jnp.bfloat16):
    loudness = shard_levels(stream_key, shape, cuts, -0.22, 0.18) if cuts else 1.0
    values = jax.random.normal(stream_key, shape, jnp.float32) * width * loudness
    return jnp.minimum(jnp.maximum(values, -bound), bound).astype(kind)


def gaussian_with(own_key, extent, width, limit, pieces, heavy, kind=jnp.bfloat16):
    array = width * jax.random.normal(own_key, extent, jnp.float32)
    if pieces:
        array = array * shard_levels(own_key, extent, pieces, -0.22, 0.18)
    return jnp.clip(raised(array, jax.random.fold_in(own_key, 3), *heavy), -limit, limit).astype(kind)


def setup_inputs(seed: int = 0) -> dict:
    streams_of = jax.random.split(jax.random.key(seed), 10)
    resid = normal_values(streams_of[0], (2, B, D), 1.0, 6.0, ((2, 512),))
    query = draw_query(jax.random.fold_in(streams_of[9], 71), 0)
    new_kv = normal_values(streams_of[2], (2, B, 2 * HD), 1.0, 6.0, ((1, 16),))
    key_cache = draw_key_cache(jax.random.fold_in(streams_of[9], 71), 0)
    value_cache = normal_values(streams_of[4], (B, SEQ, HD), 1.0, 6.0, ((0, 16), (1, 32)))
    lengths = draw_lengths(jax.random.fold_in(streams_of[9], 71), 0)
    out_weight = gaussian_with(streams_of[6], (HEADS * HD, D), (HEADS * HD) ** -0.5, 0.21875, ((0, 128), (1, 4)), (0, 1, 128, 5.5))
    hidden = normal_values(streams_of[7], (2, B, FW), 1.0, 6.0, ((1, 4), (2, 128)))
    down_weight = gaussian_with(streams_of[8], (FW, D), FW ** -0.5, 0.125, ((0, 128), (1, 4)), (0, 1, 128, 5.5))
    return dict(resid=resid, query=query, new_kv=new_kv, key_cache=key_cache, value_cache=value_cache, lengths=lengths, out_weight=out_weight, hidden=hidden, down_weight=down_weight)


def attend(args):
    qrow, keys, vals, length, fresh = args
    qf = qrow.astype(jnp.float32).reshape(2, HEADS, HD)
    kf = keys.astype(jnp.float32)
    vf = vals.astype(jnp.float32)
    fresh_k = fresh[:, :HD].astype(jnp.float32)
    incoming_value = fresh[:, HD:].astype(jnp.float32)
    scale = HD ** -0.5
    position_is_present = jnp.arange(SEQ, dtype=jnp.int32) < length
    cached_score_rows = jnp.einsum('thd,pd->thp', qf, kf) * scale
    cached_score_rows = jnp.where(position_is_present[None, None, :], cached_score_rows, -1e30)
    allowed = jnp.arange(2)[None, :] <= jnp.arange(2)[:, None]
    new_scores = jnp.einsum('thd,ud->thu', qf, fresh_k) * scale
    new_scores = jnp.where(allowed[:, None, :], new_scores, -1e30)
    global_score_maximum = jnp.maximum(jnp.max(cached_score_rows, -1), jnp.max(new_scores, -1))
    cached_attention_weight = jnp.where(position_is_present[None, None, :], jnp.exp(cached_score_rows - global_score_maximum[..., None]), 0.0).astype(jnp.bfloat16)
    new_w = jnp.where(allowed[:, None, :], jnp.exp(new_scores - global_score_maximum[..., None]), 0.0).astype(jnp.bfloat16)
    total = jnp.sum(cached_attention_weight.astype(jnp.float32), -1) + jnp.sum(new_w.astype(jnp.float32), -1)
    acc = jnp.einsum('thp,pd->thd', cached_attention_weight.astype(jnp.float32), vf)
    acc = acc + jnp.einsum('thu,ud->thd', new_w.astype(jnp.float32), incoming_value)
    return (acc / total[..., None]).reshape(2, HEADS * HD).astype(jnp.bfloat16)


def reference(resid, query, new_kv, key_cache, value_cache, lengths, out_weight, hidden, down_weight):
    per_row = lax.map(attend, (jnp.transpose(query, (1, 0, 2)), key_cache, value_cache, lengths, jnp.transpose(new_kv, (1, 0, 2))))
    attn = jnp.transpose(per_row, (1, 0, 2)).reshape(2 * B, HEADS * HD)
    projected = jnp.dot(attn, out_weight, preferred_element_type=jnp.float32)
    feed = jnp.dot(hidden.reshape(2 * B, FW), down_weight, preferred_element_type=jnp.float32)
    summed = resid.reshape(2 * B, D).astype(jnp.float32) + projected + feed
    return summed.astype(jnp.bfloat16).reshape(2, B, D)
```

```python
import jax
import jax.numpy as jnp
from jax import lax
from jax.sharding import Mesh
from jax.sharding import PartitionSpec as P

HEADS = 48
HD = 256
F32 = jnp.float32
BF16 = jnp.bfloat16
GY = ("gyx", "core")
NEG = -1e30


def per_device(
    resid, query, new_kv, key_cache, value_cache, lengths, out_weight, hidden, down_weight
):
    q = query.reshape(2, 16, 4, 768).transpose(1, 2, 0, 3)
    q = lax.all_to_all(q, "gz", split_axis=0, concat_axis=0, tiled=True)
    qf = q.reshape(16, 4, 2, 3, HD).transpose(1, 0, 2, 3, 4).reshape(4, 96, HD)

    every_hidden = lax.all_gather(hidden, "gx", axis=1, tiled=True)
    feed = jnp.einsum("tbf,fc->ctb", every_hidden, down_weight, preferred_element_type=F32)

    place = lax.axis_index(("gx",) + GY)
    positions = place * 128 + jnp.arange(128, dtype=jnp.int32)
    present = (positions[None, :] < lengths[:, None])[:, None, :]
    scale = HD**-0.5
    s = jnp.einsum("bqd,bpd->bqp", qf, key_cache, preferred_element_type=F32) * scale
    s = jnp.where(present, s, NEG)
    step = (jnp.arange(96) // 3) % 2
    allowed = (jnp.arange(2)[None, :] <= step[:, None]) & (place == 0)
    sn = jnp.einsum("bqd,ubd->bqu", qf, new_kv[..., :HD], preferred_element_type=F32) * scale
    sn = jnp.where(allowed[None], sn, NEG)
    peak = jnp.maximum(jnp.max(s, -1), jnp.max(sn, -1)).astype(BF16)
    pf = peak.astype(F32)[..., None]
    w = jnp.where(present, jnp.exp(s - pf), 0.0).astype(BF16)
    wn = jnp.where(allowed[None], jnp.exp(sn - pf), 0.0).astype(BF16)
    total = jnp.sum(w.astype(F32), -1) + jnp.sum(wn.astype(F32), -1)
    acc = jnp.einsum("bqp,bpd->bqd", w, value_cache, preferred_element_type=F32)
    acc = acc + jnp.einsum("bqu,ubd->bqd", wn, new_kv[..., HD:], preferred_element_type=F32)
    total_hi = total.astype(BF16)
    total_lo = (total - total_hi.astype(F32)).astype(BF16)
    stats = jnp.stack([peak, total_hi, total_lo, jnp.zeros_like(peak)], 1)
    stats = stats.reshape(4, 4, 8, 12).transpose(0, 2, 1, 3).reshape(32, 4, 12)
    stats = jnp.pad(stats, ((0, 0), (0, 0), (0, HD - 12)))
    message = jnp.concatenate([acc.astype(BF16).reshape(32, 12, HD), stats], 1)

    message = lax.all_to_all(message, ("gx",) + GY, split_axis=0, concat_axis=0, tiled=True)
    peaks = message[:, 12, :12].astype(F32)
    totals = message[:, 13, :12].astype(F32) + message[:, 14, :12].astype(F32)
    share = jnp.exp(peaks - jnp.max(peaks, 0))
    share = share / jnp.sum(share * totals, 0)
    attn = jnp.sum(message[:, :12].astype(F32) * share[..., None], 0).astype(BF16)
    attn = attn.reshape(2, 2, 3, HD).transpose(1, 0, 2, 3).reshape(2, 16, 96).transpose(1, 0, 2)
    attn = jnp.broadcast_to(attn[:, None], (16, 4, 2, 96)).reshape(64, 2, 96)

    mine = lax.all_to_all(attn, ("gz", "gx"), split_axis=0, concat_axis=0, tiled=True)
    projected = jnp.einsum("btf,fc->ctb", mine, out_weight, preferred_element_type=F32)

    part = (projected + feed).reshape(4, 2, 576, 128)
    core = lax.axis_index("core")
    theirs = lax.dynamic_index_in_dim(part, 1 - core, 1, keepdims=False).astype(BF16)
    ours = lax.dynamic_index_in_dim(part, core, 1, keepdims=False)
    theirs = lax.ppermute(theirs, "core", [(0, 1), (1, 0)])
    pair = (ours + theirs.astype(F32)).astype(BF16)
    row = lax.all_to_all(pair, "gyx", split_axis=0, concat_axis=0, tiled=True)
    row = jnp.sum(row.astype(F32), 0).astype(BF16).reshape(16, 36, 128)
    column = lax.all_to_all(row, "gz", split_axis=0, concat_axis=0, tiled=True)
    summed = jnp.sum(column.astype(F32), 0).reshape(36, 2, 64).transpose(1, 2, 0)
    return (summed + resid.astype(F32)).astype(BF16)


def solution(mesh):
    mesh = Mesh(mesh.devices.reshape(4, 4, 2, 16), ("gx", "gyx", "core", "gz"))
    rows = GY + ("gz",)
    width = P(None, None, ("gx",) + rows)
    in_specs = (
        width,
        P(None, None, "gz"),
        P(None, "gz", None),
        P("gz", ("gx",) + GY, None),
        P("gz", ("gx",) + GY, None),
        P("gz"),
        P(rows, "gx"),
        P(None, "gx", rows),
        P(rows, "gx"),
    )
    return jax.shard_map(
        per_device, mesh=mesh, in_specs=in_specs, out_specs=width, check_vma=False
    )
```

```python
import jax
import jax.numpy as jnp
from jax import lax
from jax.experimental import pallas as pl
from jax.experimental.pallas import tpu as pltpu
from jax.sharding import Mesh
from jax.sharding import PartitionSpec as P

HEADS = 48
HD = 256
F32 = jnp.float32
BF16 = jnp.bfloat16
GY = ("gyx", "core")
NEG = -1e30
TILE = 1152


def turned_product(x, w, dtype, more=None):
    rows, depth = x.shape
    columns = w.shape[1]

    def kernel(x_ref, w_ref, *refs):
        y = jnp.dot(x_ref[...], w_ref[...], preferred_element_type=F32).T
        if more is not None:
            y = y + refs[0][...]
        refs[-1][...] = y.astype(dtype)

    out_block = pl.BlockSpec((TILE, rows), lambda i: (i, 0))
    in_specs = [
        pl.BlockSpec((rows, depth), lambda i: (0, 0)),
        pl.BlockSpec((depth, TILE), lambda i: (0, i)),
    ]
    operands = [x, w]
    if more is not None:
        in_specs.append(out_block)
        operands.append(more)
    return pl.pallas_call(
        kernel,
        grid=(columns // TILE,),
        in_specs=in_specs,
        out_specs=out_block,
        out_shape=jax.ShapeDtypeStruct((columns, rows), dtype),
        compiler_params=pltpu.CompilerParams(vmem_limit_bytes=16 * 2**20),
        cost_estimate=pl.CostEstimate(
            flops=2 * rows * depth * columns,
            bytes_accessed=2 * depth * columns + 4 * rows * columns,
            transcendentals=0,
        ),
    )(*operands)


def exchange(x, axes):
    return lax.all_to_all(x, axes, split_axis=0, concat_axis=0, tiled=True)


def per_device(
    resid, query, new_kv, key_cache, value_cache, lengths, out_weight, hidden, down_weight
):
    gx = lax.axis_index("gx")
    gy = lax.axis_index(GY)
    blocks = []
    for hop in range(4):
        owner = (gx + hop) & 3
        block = jnp.concatenate(
            [lax.dynamic_index_in_dim(c, owner, 0, False) for c in (key_cache, value_cache)], -1
        )
        if hop:
            block = lax.ppermute(block, "gx", [(i, (i + hop) % 4) for i in range(4)])
        blocks.append(block)
    cache = jnp.concatenate(blocks, 0)
    keys, values = cache[:, :HD], cache[:, HD:]

    pick = jnp.arange(32)
    pick = (pick % 2) * 64 + (pick // 2) * 4 + gx
    pick = (pick[:, None] == jnp.arange(128)[None, :]).astype(BF16)
    q = jnp.dot(pick, query.reshape(128, 768), preferred_element_type=F32).astype(BF16)
    q = exchange(q.reshape(16, 2, 768), "gz")
    qf = q.reshape(16, 2, 3, HD).reshape(96, HD)

    at = jnp.arange(512, dtype=jnp.int32)
    positions = (((gx - at // 128) & 3) * 8 + gy) * 128 + at % 128
    length = lax.dynamic_index_in_dim(lengths, gx, 0, keepdims=False)
    present = (positions < length)[None]
    scale = HD**-0.5
    s = jnp.einsum("qd,pd->qp", qf, keys, preferred_element_type=F32) * scale
    s = jnp.where(present, s, NEG)
    fresh = lax.dynamic_index_in_dim(new_kv, gx, 1, keepdims=False)
    step = (jnp.arange(96) // 3) % 2
    allowed = (jnp.arange(2)[None, :] <= step[:, None]) & (gy == 0)
    sn = jnp.einsum("qd,ud->qu", qf, fresh[:, :HD], preferred_element_type=F32) * scale
    sn = jnp.where(allowed, sn, NEG)
    peak = jnp.maximum(jnp.max(s, -1), jnp.max(sn, -1)).astype(BF16)
    pf = peak.astype(F32)[:, None]
    w = jnp.where(present, jnp.exp(s - pf), 0.0).astype(BF16)
    wn = jnp.where(allowed, jnp.exp(sn - pf), 0.0).astype(BF16)
    total = jnp.sum(w.astype(F32), -1) + jnp.sum(wn.astype(F32), -1)
    acc = jnp.einsum("qp,pd->qd", w, values, preferred_element_type=F32)
    acc = acc + jnp.einsum("qu,ud->qd", wn, fresh[:, HD:], preferred_element_type=F32)
    total_hi = total.astype(BF16)
    total_lo = (total - total_hi.astype(F32)).astype(BF16)
    stats = jnp.stack([peak, total_hi, total_lo, jnp.zeros_like(peak)], 0)
    stats = stats.reshape(4, 8, 12).transpose(1, 0, 2)
    stats = jnp.pad(stats, ((0, 0), (0, 0), (0, HD - 12)))
    message = jnp.concatenate([acc.astype(BF16).reshape(8, 12, HD), stats], 1)

    message = exchange(message, GY)
    peaks = message[:, 12, :12].astype(F32)
    totals = message[:, 13, :12].astype(F32) + message[:, 14, :12].astype(F32)
    share = jnp.exp(peaks - jnp.max(peaks, 0))
    share = share / jnp.sum(share * totals, 0)
    attn = jnp.sum(message[:, :12].astype(F32) * share[..., None], 0).astype(BF16)
    attn = attn.reshape(2, 2, 3, HD).transpose(1, 0, 2, 3).reshape(2, 16, 96).transpose(1, 0, 2)
    attn = jnp.broadcast_to(attn[:, None], (16, 4, 2, 96)).reshape(64, 2, 96)

    spread = lax.all_gather(hidden, "gx", axis=1, tiled=True).reshape(128, 288)
    feed = turned_product(spread, down_weight, F32)

    mine = exchange(attn, ("gz", "gx")).transpose(1, 0, 2).reshape(128, 96)
    part = turned_product(mine, out_weight, BF16, feed)

    row = exchange(part.reshape(8, 576, 128), GY)
    row = jnp.sum(row.astype(F32), 0).astype(BF16).reshape(16, 36, 128)
    column = exchange(row, "gz")
    summed = jnp.sum(column.astype(F32), 0).reshape(36, 2, 64).transpose(1, 2, 0)
    return (summed + resid.astype(F32)).astype(BF16)


def solution(mesh):
    mesh = Mesh(mesh.devices.reshape(4, 4, 2, 16), ("gx", "gyx", "core", "gz"))
    rows = GY + ("gz",)
    width = P(None, None, ("gx",) + rows)
    in_specs = (
        width,
        P(None, None, "gz"),
        P(None, "gz", None),
        P("gz", ("gx",) + GY, None),
        P("gz", ("gx",) + GY, None),
        P("gz"),
        P(rows, "gx"),
        P(None, "gx", rows),
        P(rows, "gx"),
    )
    return jax.shard_map(
        per_device, mesh=mesh, in_specs=in_specs, out_specs=width, check_vma=False
    )
```

```python
import jax
import jax.numpy as jnp
from jax import lax
from jax.experimental import pallas as pl
from jax.experimental.pallas import tpu as pltpu
from jax.sharding import Mesh
from jax.sharding import PartitionSpec as P

HEADS = 48
HD = 256
F32 = jnp.float32
BF16 = jnp.bfloat16
GY = ("gyx", "core")
NEG = -1e30
TILE = 1152


def split_product(core, x, out_weight, gathered, down_weight):
    rows, depth = x.shape
    shares, held, width = gathered.shape
    columns = out_weight.shape[1]
    half = TILE // 2

    def kernel(core_ref, x_ref, w_ref, h_ref, d_ref, ours_ref, theirs_ref, full_ref):
        hidden = jnp.concatenate(
            [h_ref[s, 16 * t : 16 * t + 16, :] for t in range(2) for s in range(shares)], 0
        )
        y = jnp.dot(hidden, d_ref[...], preferred_element_type=F32)
        y = y + jnp.dot(x_ref[...], w_ref[...], preferred_element_type=F32)
        full_ref[...] = y.T
        mine = core_ref[0]
        ours_ref[...] = full_ref[pl.ds(pl.multiple_of(mine * half, half), half), :]
        theirs = full_ref[pl.ds(pl.multiple_of((1 - mine) * half, half), half), :]
        theirs_ref[...] = theirs.astype(BF16)

    half_block = pl.BlockSpec((half, rows), lambda i: (i, 0))
    return pl.pallas_call(
        kernel,
        grid=(columns // TILE,),
        in_specs=[
            pl.BlockSpec(memory_space=pltpu.SMEM),
            pl.BlockSpec((rows, depth), lambda i: (0, 0)),
            pl.BlockSpec((depth, TILE), lambda i: (0, i)),
            pl.BlockSpec((shares, held, width), lambda i: (0, 0, 0)),
            pl.BlockSpec((width, TILE), lambda i: (0, i)),
        ],
        out_specs=[half_block, half_block],
        out_shape=[
            jax.ShapeDtypeStruct((columns // 2, rows), F32),
            jax.ShapeDtypeStruct((columns // 2, rows), BF16),
        ],
        scratch_shapes=[pltpu.VMEM((TILE, rows), F32)],
        compiler_params=pltpu.CompilerParams(vmem_limit_bytes=16 * 2**20),
        cost_estimate=pl.CostEstimate(
            flops=2 * rows * (depth + width) * columns,
            bytes_accessed=2 * (depth + width) * columns + 3 * rows * columns,
            transcendentals=0,
        ),
    )(core.reshape(1), x, out_weight, gathered, down_weight)


def exchange(x, axes):
    return lax.all_to_all(x, axes, split_axis=0, concat_axis=0, tiled=True)


def per_device(
    resid, query, new_kv, key_cache, value_cache, lengths, out_weight, hidden, down_weight
):
    gx, gyx, core = lax.axis_index("gx"), lax.axis_index("gyx"), lax.axis_index("core")

    spread = jnp.pad(hidden.reshape(32, 288), ((0, 480), (0, 0)))
    spread = lax.all_gather(spread, "gx", axis=0, tiled=True).reshape(4, 512, 288)[:, :32]

    pair = jnp.concatenate([key_cache, value_cache], -1)
    pair = lax.ppermute(pair, "core", [(0, 1), (1, 0)])
    keys = jnp.concatenate([key_cache, pair[..., :HD]], 1)
    values = jnp.concatenate([value_cache, pair[..., HD:]], 1)
    q = exchange(query.reshape(2, 16, 4, 768).transpose(1, 2, 0, 3), "gz")
    q = lax.dynamic_index_in_dim(q.reshape(4, 2, 2, 4, 2, 768), core, 1, keepdims=False)
    qf = q.reshape(4, 2, 4, 2, 3, HD).transpose(2, 0, 1, 3, 4, 5).reshape(4, 48, HD)

    at = jnp.arange(256, dtype=jnp.int32)
    owner = gx * 8 + gyx * 2 + jnp.where(at < 128, core, 1 - core)
    positions = owner * 128 + at % 128
    present = (positions[None] < lengths[:, None])[:, None]
    scale = HD**-0.5
    s = jnp.einsum("bqd,bpd->bqp", qf, keys, preferred_element_type=F32) * scale
    s = jnp.where(present, s, NEG)
    step = (jnp.arange(48) // 3) % 2
    allowed = (jnp.arange(2)[None, :] <= step[:, None]) & (gx + gyx == 0)
    sn = jnp.einsum("bqd,ubd->bqu", qf, new_kv[..., :HD], preferred_element_type=F32) * scale
    sn = jnp.where(allowed, sn, NEG)
    peak = jnp.maximum(jnp.max(s, -1), jnp.max(sn, -1)).astype(BF16)
    pf = peak.astype(F32)[..., None]
    w = jnp.where(present, jnp.exp(s - pf), 0.0).astype(BF16)
    wn = jnp.where(allowed, jnp.exp(sn - pf), 0.0).astype(BF16)
    total = jnp.sum(w.astype(F32), -1) + jnp.sum(wn.astype(F32), -1)
    acc = jnp.einsum("bqp,bpd->bqd", w, values, preferred_element_type=F32)
    acc = acc + jnp.einsum("bqu,ubd->bqd", wn, new_kv[..., HD:], preferred_element_type=F32)
    total_hi = total.astype(BF16)
    total_lo = (total - total_hi.astype(F32)).astype(BF16)
    stats = jnp.stack([peak, total_hi, total_lo, jnp.zeros_like(peak)], 1)
    stats = stats.reshape(4, 4, 4, 12).transpose(0, 2, 1, 3).reshape(16, 4, 12)
    stats = jnp.pad(stats, ((0, 0), (0, 0), (0, HD - 12)))
    message = jnp.concatenate([acc.astype(BF16).reshape(16, 12, HD), stats], 1)

    message = exchange(message, ("gx", "gyx"))
    peaks = message[:, 12, :12].astype(F32)
    totals = message[:, 13, :12].astype(F32) + message[:, 14, :12].astype(F32)
    share = jnp.exp(peaks - jnp.max(peaks, 0))
    share = share / jnp.sum(share * totals, 0)
    attn = jnp.sum(message[:, :12].astype(F32) * share[..., None], 0).astype(BF16)
    attn = attn.reshape(2, 2, 3, HD).transpose(1, 0, 2, 3).reshape(2, 16, 96).transpose(1, 0, 2)
    attn = jnp.broadcast_to(attn[:, None], (16, 4, 2, 96)).reshape(64, 2, 96)

    attn, spread = lax.optimization_barrier((attn, spread))

    mine = exchange(attn, ("gz", "gx")).transpose(1, 0, 2).reshape(128, 96)
    ours, theirs = split_product(core, mine, out_weight, spread, down_weight)

    theirs = lax.ppermute(theirs, "core", [(0, 1), (1, 0)])
    row = (ours + theirs.astype(F32)).astype(BF16).reshape(4, 576, 128)
    row = exchange(row, "gyx")
    row = jnp.sum(row.astype(F32), 0).astype(BF16).reshape(16, 36, 128)
    column = exchange(row, "gz")
    summed = jnp.sum(column.astype(F32), 0).reshape(36, 2, 64).transpose(1, 2, 0)
    return (summed + resid.astype(F32)).astype(BF16)


def solution(mesh):
    mesh = Mesh(mesh.devices.reshape(4, 4, 2, 16), ("gx", "gyx", "core", "gz"))
    rows = GY + ("gz",)
    width = P(None, None, ("gx",) + rows)
    in_specs = (
        width,
        P(None, None, "gz"),
        P(None, "gz", None),
        P("gz", ("gx",) + GY, None),
        P("gz", ("gx",) + GY, None),
        P("gz"),
        P(rows, "gx"),
        P(None, "gx", rows),
        P(rows, "gx"),
    )
    return jax.shard_map(
        per_device, mesh=mesh, in_specs=in_specs, out_specs=width, check_vma=False
    )
```

```python
import jax
import jax.numpy as jnp
from jax import lax
from jax.experimental import pallas as pl
from jax.experimental.pallas import tpu as pltpu
from jax.sharding import Mesh
from jax.sharding import PartitionSpec as P

HEADS = 48
HD = 256
F32 = jnp.float32
BF16 = jnp.bfloat16
GY = ("gyx", "core")
NEG = -1e30
TILE = 1152


def split_product(core, x, out_weight, gathered, down_weight):
    rows, depth = x.shape
    shares, held, width = gathered.shape
    columns = out_weight.shape[1]
    half = TILE // 2

    tiles = columns // TILE

    def kernel(core_ref, x_ref, h_ref, w_hbm, d_hbm, ours_ref, theirs_ref, w_buf, d_buf, full, sems):
        copies = []
        for i in range(tiles):
            place = pl.ds(i * TILE, TILE)
            copies.append(
                (
                    pltpu.make_async_copy(d_hbm.at[:, place], d_buf.at[i], sems.at[0, i]),
                    pltpu.make_async_copy(w_hbm.at[:, place], w_buf.at[i], sems.at[1, i]),
                )
            )
            for copy in copies[-1]:
                copy.start()
        hidden = jnp.concatenate(
            [h_ref[s, 16 * t : 16 * t + 16, :] for t in range(2) for s in range(shares)], 0
        )
        mine = core_ref[0]
        for i in range(tiles):
            for copy in copies[i]:
                copy.wait()
            y = jnp.dot(hidden, d_buf[i], preferred_element_type=F32)
            y = y + jnp.dot(x_ref[...], w_buf[i], preferred_element_type=F32)
            full[...] = y.T
            rows_i = pl.ds(i * half, half)
            ours_ref[rows_i, :] = full[pl.ds(pl.multiple_of(mine * half, half), half), :]
            theirs = full[pl.ds(pl.multiple_of((1 - mine) * half, half), half), :]
            theirs_ref[rows_i, :] = theirs.astype(BF16)

    in_vmem = pl.BlockSpec(memory_space=pltpu.VMEM)
    in_hbm = pl.BlockSpec(memory_space=pltpu.HBM)
    return pl.pallas_call(
        kernel,
        in_specs=[pl.BlockSpec(memory_space=pltpu.SMEM), in_vmem, in_vmem, in_hbm, in_hbm],
        out_specs=[in_vmem, in_vmem],
        out_shape=[
            jax.ShapeDtypeStruct((columns // 2, rows), F32),
            jax.ShapeDtypeStruct((columns // 2, rows), BF16),
        ],
        scratch_shapes=[
            pltpu.VMEM((tiles, depth, TILE), BF16),
            pltpu.VMEM((tiles, width, TILE), BF16),
            pltpu.VMEM((TILE, rows), F32),
            pltpu.SemaphoreType.DMA((2, tiles)),
        ],
        compiler_params=pltpu.CompilerParams(vmem_limit_bytes=51 * 2**20),
        cost_estimate=pl.CostEstimate(
            flops=2 * rows * (depth + width) * columns,
            bytes_accessed=2 * (depth + width) * columns + 3 * rows * columns,
            transcendentals=0,
        ),
    )(core.reshape(1), x, gathered, out_weight, down_weight)


def exchange(x, axes):
    return lax.all_to_all(x, axes, split_axis=0, concat_axis=0, tiled=True)


def per_device(
    resid, query, new_kv, key_cache, value_cache, lengths, out_weight, hidden, down_weight
):
    gx, gyx, core = lax.axis_index("gx"), lax.axis_index("gyx"), lax.axis_index("core")

    pair = jnp.concatenate([key_cache, value_cache], -1)
    pair, own = lax.optimization_barrier((pair, hidden))
    pair = lax.ppermute(pair, "core", [(0, 1), (1, 0)])
    near = lax.ppermute(own, "gx", [(i, i ^ 1) for i in range(4)])
    keys = jnp.concatenate([key_cache, pair[..., :HD]], 1)
    values = jnp.concatenate([value_cache, pair[..., HD:]], 1)
    keys, near = lax.optimization_barrier((keys, near))
    near = jnp.where(gx % 2 == 0, jnp.stack([hidden, near]), jnp.stack([near, hidden]))
    far = lax.ppermute(near, "gx", [(i, i ^ 2) for i in range(4)])
    q = exchange(query.reshape(2, 16, 4, 768).transpose(1, 2, 0, 3), "gz")
    q = lax.dynamic_index_in_dim(q.reshape(4, 2, 2, 4, 2, 768), core, 1, keepdims=False)
    qf = q.reshape(4, 2, 4, 2, 3, HD).transpose(2, 0, 1, 3, 4, 5).reshape(4, 48, HD)

    at = jnp.arange(256, dtype=jnp.int32)
    owner = gx * 8 + gyx * 2 + jnp.where(at < 128, core, 1 - core)
    positions = owner * 128 + at % 128
    present = (positions[None] < lengths[:, None])[:, None]
    scale = HD**-0.5
    s = jnp.einsum("bqd,bpd->bqp", qf, keys, preferred_element_type=F32) * scale
    s = jnp.where(present, s, NEG)
    step = (jnp.arange(48) // 3) % 2
    allowed = (jnp.arange(2)[None, :] <= step[:, None]) & (gx + gyx == 0)
    sn = jnp.einsum("bqd,ubd->bqu", qf, new_kv[..., :HD], preferred_element_type=F32) * scale
    sn = jnp.where(allowed, sn, NEG)
    peak = jnp.maximum(jnp.max(s, -1), jnp.max(sn, -1)).astype(BF16)
    pf = peak.astype(F32)[..., None]
    w = jnp.where(present, jnp.exp(s - pf), 0.0).astype(BF16)
    wn = jnp.where(allowed, jnp.exp(sn - pf), 0.0).astype(BF16)
    total = jnp.sum(w.astype(F32), -1) + jnp.sum(wn.astype(F32), -1)
    acc = jnp.einsum("bqp,bpd->bqd", w, values, preferred_element_type=F32)
    acc = acc + jnp.einsum("bqu,ubd->bqd", wn, new_kv[..., HD:], preferred_element_type=F32)
    total_hi = total.astype(BF16)
    total_lo = (total - total_hi.astype(F32)).astype(BF16)
    stats = jnp.stack([peak, total_hi, total_lo, jnp.zeros_like(peak)], 1)
    stats = stats.reshape(4, 4, 4, 12).transpose(0, 2, 1, 3).reshape(16, 4, 12)
    stats = jnp.pad(stats, ((0, 0), (0, 0), (0, HD - 12)))
    message = jnp.concatenate([acc.astype(BF16).reshape(16, 12, HD), stats], 1)

    message = exchange(message, ("gx", "gyx"))
    peaks = message[:, 12, :12].astype(F32)
    totals = message[:, 13, :12].astype(F32) + message[:, 14, :12].astype(F32)
    share = jnp.exp(peaks - jnp.max(peaks, 0))
    share = share / jnp.sum(share * totals, 0)
    attn = jnp.sum(message[:, :12].astype(F32) * share[..., None], 0).astype(BF16)
    attn = attn.reshape(2, 2, 3, HD).transpose(1, 0, 2, 3).reshape(2, 16, 96).transpose(1, 0, 2)
    attn = jnp.broadcast_to(attn[:, None], (16, 4, 2, 96)).reshape(64, 2, 96)

    attn, far = lax.optimization_barrier((attn, far))
    spread = jnp.where(gx < 2, jnp.concatenate([near, far]), jnp.concatenate([far, near]))
    spread = spread.reshape(4, 32, 288)

    mine = exchange(attn, ("gz", "gx")).transpose(1, 0, 2).reshape(128, 96)
    ours, theirs = split_product(core, mine, out_weight, spread, down_weight)

    theirs = lax.ppermute(theirs, "core", [(0, 1), (1, 0)])
    row = (ours + theirs.astype(F32)).astype(BF16).reshape(4, 576, 128)
    row = exchange(row, "gyx")
    row = jnp.sum(row.astype(F32), 0).astype(BF16).reshape(16, 36, 128)
    column = exchange(row, "gz")
    summed = jnp.sum(column.astype(F32), 0).reshape(36, 2, 64).transpose(1, 2, 0)
    return (summed + resid.astype(F32)).astype(BF16)


def solution(mesh):
    mesh = Mesh(mesh.devices.reshape(4, 4, 2, 16), ("gx", "gyx", "core", "gz"))
    rows = GY + ("gz",)
    width = P(None, None, ("gx",) + rows)
    in_specs = (
        width,
        P(None, None, "gz"),
        P(None, "gz", None),
        P("gz", ("gx",) + GY, None),
        P("gz", ("gx",) + GY, None),
        P("gz"),
        P(rows, "gx"),
        P(None, "gx", rows),
        P(rows, "gx"),
    )
    return jax.shard_map(
        per_device, mesh=mesh, in_specs=in_specs, out_specs=width, check_vma=False
    )
```

```python
import jax
import jax.numpy as jnp
from jax import lax
from jax.experimental import pallas as pl
from jax.experimental.pallas import tpu as pltpu
from jax.sharding import Mesh
from jax.sharding import PartitionSpec as P

HEADS = 48
HD = 256
F32 = jnp.float32
BF16 = jnp.bfloat16
GY = ("gyx", "core")
NEG = -1e30
TILE = 1152


def turned_product(gathered, w):
    shares, held, width = gathered.shape
    rows = shares * held
    columns = w.shape[1]
    tiles = columns // TILE

    def kernel(h_ref, w_hbm, o_ref, w_buf, sems):
        copies = []
        for i in range(tiles):
            place = pl.ds(i * TILE, TILE)
            copies.append(pltpu.make_async_copy(w_hbm.at[:, place], w_buf.at[i], sems.at[i]))
            copies[-1].start()
        hidden = jnp.concatenate(
            [h_ref[s, 16 * t : 16 * t + 16, :] for t in range(2) for s in range(shares)], 0
        )
        for i in range(tiles):
            copies[i].wait()
            y = jnp.dot(hidden, w_buf[i], preferred_element_type=F32)
            o_ref[pl.ds(i * TILE, TILE), :] = y.T

    in_vmem = pl.BlockSpec(memory_space=pltpu.VMEM)
    return pl.pallas_call(
        kernel,
        in_specs=[in_vmem, pl.BlockSpec(memory_space=pltpu.HBM)],
        out_specs=in_vmem,
        out_shape=jax.ShapeDtypeStruct((columns, rows), F32),
        scratch_shapes=[
            pltpu.VMEM((tiles, width, TILE), BF16),
            pltpu.SemaphoreType.DMA((tiles,)),
        ],
        compiler_params=pltpu.CompilerParams(vmem_limit_bytes=51 * 2**20),
        cost_estimate=pl.CostEstimate(
            flops=2 * rows * width * columns,
            bytes_accessed=2 * width * columns + 4 * rows * columns,
            transcendentals=0,
        ),
    )(gathered, w)


def split_product(place, xs, weights, more):
    many, rows, depth = xs.shape
    half = TILE // 2

    def kernel(place_ref, x_ref, *refs):
        w_refs, (more_ref, ours_ref, theirs_ref, full) = refs[:many], refs[many:]
        chip, mine = place_ref[0], place_ref[1]
        y = jnp.dot(x_ref[chip], w_refs[0][...], preferred_element_type=F32)
        for j in range(1, many):
            x = x_ref[lax.rem(chip + (many - j), many)]
            y = y + jnp.dot(x, w_refs[j][...], preferred_element_type=F32)
        full[...] = y.T + more_ref[...]
        ours_ref[...] = full[pl.ds(pl.multiple_of(mine * half, half), half), :]
        theirs = full[pl.ds(pl.multiple_of((1 - mine) * half, half), half), :]
        theirs_ref[...] = theirs.astype(BF16)

    in_vmem = pl.BlockSpec(memory_space=pltpu.VMEM)
    return pl.pallas_call(
        kernel,
        in_specs=[pl.BlockSpec(memory_space=pltpu.SMEM)] + [in_vmem] * (many + 2),
        out_specs=[in_vmem, in_vmem],
        out_shape=[
            jax.ShapeDtypeStruct((half, rows), F32),
            jax.ShapeDtypeStruct((half, rows), BF16),
        ],
        scratch_shapes=[pltpu.VMEM((TILE, rows), F32)],
        compiler_params=pltpu.CompilerParams(vmem_limit_bytes=16 * 2**20),
        cost_estimate=pl.CostEstimate(
            flops=2 * rows * depth * many * TILE,
            bytes_accessed=2 * depth * many * TILE + 7 * rows * TILE,
            transcendentals=0,
        ),
    )(place, xs, *weights, more)


def exchange(x, axes):
    return lax.all_to_all(x, axes, split_axis=0, concat_axis=0, tiled=True)


def per_device(
    resid, query, new_kv, key_cache, value_cache, lengths, out_weight, hidden, down_weight
):
    gx, gyx, core = lax.axis_index("gx"), lax.axis_index("gyx"), lax.axis_index("core")

    pair = jnp.concatenate([key_cache, value_cache], -1)
    pair, own = lax.optimization_barrier((pair, hidden))
    pair = lax.ppermute(pair, "core", [(0, 1), (1, 0)])
    near = lax.ppermute(own, "gx", [(i, i ^ 1) for i in range(4)])
    keys = jnp.concatenate([key_cache, pair[..., :HD]], 1)
    values = jnp.concatenate([value_cache, pair[..., HD:]], 1)
    near = jnp.where(gx % 2 == 0, jnp.stack([hidden, near]), jnp.stack([near, hidden]))
    far = lax.ppermute(near, "gx", [(i, i ^ 2) for i in range(4)])
    keys, near, far = lax.optimization_barrier((keys, near, far))
    spread = jnp.where(gx < 2, jnp.concatenate([near, far]), jnp.concatenate([far, near]))
    feed = turned_product(spread.reshape(4, 32, 288), down_weight)
    q = exchange(query.reshape(2, 16, 4, 768).transpose(1, 2, 0, 3), "gz")
    q = lax.dynamic_index_in_dim(q.reshape(4, 2, 2, 4, 2, 768), core, 1, keepdims=False)
    qf = q.reshape(4, 2, 4, 2, 3, HD).transpose(2, 0, 1, 3, 4, 5).reshape(4, 48, HD)

    at = jnp.arange(256, dtype=jnp.int32)
    owner = gx * 8 + gyx * 2 + jnp.where(at < 128, core, 1 - core)
    positions = owner * 128 + at % 128
    present = (positions[None] < lengths[:, None])[:, None]
    scale = HD**-0.5
    s = jnp.einsum("bqd,bpd->bqp", qf, keys, preferred_element_type=F32) * scale
    s = jnp.where(present, s, NEG)
    step = (jnp.arange(48) // 3) % 2
    allowed = (jnp.arange(2)[None, :] <= step[:, None]) & (gx + gyx == 0)
    sn = jnp.einsum("bqd,ubd->bqu", qf, new_kv[..., :HD], preferred_element_type=F32) * scale
    sn = jnp.where(allowed, sn, NEG)
    peak = jnp.maximum(jnp.max(s, -1), jnp.max(sn, -1)).astype(BF16)
    pf = peak.astype(F32)[..., None]
    w = jnp.where(present, jnp.exp(s - pf), 0.0).astype(BF16)
    wn = jnp.where(allowed, jnp.exp(sn - pf), 0.0).astype(BF16)
    total = jnp.sum(w.astype(F32), -1) + jnp.sum(wn.astype(F32), -1)
    acc = jnp.einsum("bqp,bpd->bqd", w, values, preferred_element_type=F32)
    acc = acc + jnp.einsum("bqu,ubd->bqd", wn, new_kv[..., HD:], preferred_element_type=F32)
    total_hi = total.astype(BF16)
    total_lo = (total - total_hi.astype(F32)).astype(BF16)
    stats = jnp.stack([peak, total_hi, total_lo, jnp.zeros_like(peak)], 1)
    stats = stats.reshape(4, 4, 4, 12).transpose(0, 2, 1, 3).reshape(16, 4, 12)
    stats = jnp.pad(stats, ((0, 0), (0, 0), (0, HD - 12)))
    message = jnp.concatenate([acc.astype(BF16).reshape(16, 12, HD), stats], 1)

    message = exchange(message, ("gx", "gyx"))
    peaks = message[:, 12, :12].astype(F32)
    totals = message[:, 13, :12].astype(F32) + message[:, 14, :12].astype(F32)
    share = jnp.exp(peaks - jnp.max(peaks, 0))
    share = share / jnp.sum(share * totals, 0)
    attn = jnp.sum(message[:, :12].astype(F32) * share[..., None], 0).astype(BF16)
    attn = attn.reshape(2, 2, 3, HD).transpose(1, 0, 2, 3).reshape(2, 16, 96).transpose(1, 0, 2)

    weights = [
        lax.dynamic_slice_in_dim(out_weight, ((gyx + hop) & 3) * TILE, TILE, 1) for hop in range(4)
    ]
    feed_sum = lax.psum_scatter(feed, "gyx", scatter_dimension=0, tiled=True)
    attn, feed, *weights = lax.optimization_barrier((attn, feed, *weights))
    for hop in range(1, 4):
        weights[hop] = lax.ppermute(weights[hop], "gyx", [(i, (i + hop) % 4) for i in range(4)])

    attn = exchange(jnp.pad(attn, ((0, 0), (0, 14), (0, 160))), "gz")[:, :2, :96]
    place = jnp.stack([gyx, core])
    attn, place, *weights = lax.optimization_barrier((attn, place, *weights))
    attn = exchange(jnp.broadcast_to(attn[None], (16, 16, 2, 96)), ("gx", "gyx"))
    attn = attn.reshape(4, 4, 16, 2, 96).transpose(1, 3, 2, 0, 4).reshape(4, 128, 96)
    ours, theirs = split_product(place, attn, weights, feed_sum)

    theirs = lax.ppermute(theirs, "core", [(0, 1), (1, 0)])
    row = (ours + theirs.astype(F32)).astype(BF16).reshape(16, 36, 128)
    column = exchange(row, "gz")
    summed = jnp.sum(column.astype(F32), 0).reshape(36, 2, 64).transpose(1, 2, 0)
    return (summed + resid.astype(F32)).astype(BF16)


def solution(mesh):
    mesh = Mesh(mesh.devices.reshape(4, 4, 2, 16), ("gx", "gyx", "core", "gz"))
    rows = GY + ("gz",)
    width = P(None, None, ("gx",) + rows)
    in_specs = (
        width,
        P(None, None, "gz"),
        P(None, "gz", None),
        P("gz", ("gx",) + GY, None),
        P("gz", ("gx",) + GY, None),
        P("gz"),
        P(rows, "gx"),
        P(None, "gx", rows),
        P(rows, "gx"),
    )
    return jax.shard_map(
        per_device, mesh=mesh, in_specs=in_specs, out_specs=width, check_vma=False
    )
```

```python
import jax
import jax.numpy as jnp
from jax import lax
from jax.experimental import pallas as pl
from jax.experimental.pallas import tpu as pltpu
from jax.sharding import Mesh
from jax.sharding import PartitionSpec as P

HEADS = 48
HD = 256
F32 = jnp.float32
BF16 = jnp.bfloat16
GY = ("gyx", "core")
NEG = -1e30
TILE = 1152


def turned_product(gathered, w):
    shares, held, width = gathered.shape
    rows = shares * held
    columns = w.shape[1]
    tiles = columns // TILE

    def kernel(h_ref, w_hbm, o_ref, w_buf, sems):
        copies = []
        for i in range(tiles):
            place = pl.ds(i * TILE, TILE)
            copies.append(pltpu.make_async_copy(w_hbm.at[:, place], w_buf.at[i], sems.at[i]))
            copies[-1].start()
        hidden = jnp.concatenate(
            [h_ref[s, 16 * t : 16 * t + 16, :] for t in range(2) for s in range(shares)], 0
        )
        for i in range(tiles):
            copies[i].wait()
            y = jnp.dot(hidden, w_buf[i], preferred_element_type=F32)
            o_ref[pl.ds(i * TILE, TILE), :] = y.T

    in_vmem = pl.BlockSpec(memory_space=pltpu.VMEM)
    return pl.pallas_call(
        kernel,
        in_specs=[in_vmem, pl.BlockSpec(memory_space=pltpu.HBM)],
        out_specs=in_vmem,
        out_shape=jax.ShapeDtypeStruct((columns, rows), F32),
        scratch_shapes=[
            pltpu.VMEM((tiles, width, TILE), BF16),
            pltpu.SemaphoreType.DMA((tiles,)),
        ],
        compiler_params=pltpu.CompilerParams(vmem_limit_bytes=51 * 2**20),
        cost_estimate=pl.CostEstimate(
            flops=2 * rows * width * columns,
            bytes_accessed=2 * width * columns + 4 * rows * columns,
            transcendentals=0,
        ),
    )(gathered, w)


def split_product(core, x, w, more):
    rows, depth = x.shape
    columns = w.shape[1]
    half = TILE // 2

    def kernel(core_ref, x_ref, w_ref, more_ref, ours_ref, theirs_ref, full):
        mine = core_ref[0]
        for i in range(columns // TILE):
            place = pl.ds(i * TILE, TILE)
            y = jnp.dot(x_ref[...], w_ref[:, place], preferred_element_type=F32)
            full[...] = y.T + more_ref[place, :]
            rows_i = pl.ds(i * half, half)
            ours_ref[rows_i, :] = full[pl.ds(pl.multiple_of(mine * half, half), half), :]
            theirs = full[pl.ds(pl.multiple_of((1 - mine) * half, half), half), :]
            theirs_ref[rows_i, :] = theirs.astype(BF16)

    in_vmem = pl.BlockSpec(memory_space=pltpu.VMEM)
    return pl.pallas_call(
        kernel,
        in_specs=[pl.BlockSpec(memory_space=pltpu.SMEM), in_vmem, in_vmem, in_vmem],
        out_specs=[in_vmem, in_vmem],
        out_shape=[
            jax.ShapeDtypeStruct((columns // 2, rows), F32),
            jax.ShapeDtypeStruct((columns // 2, rows), BF16),
        ],
        scratch_shapes=[pltpu.VMEM((TILE, rows), F32)],
        compiler_params=pltpu.CompilerParams(vmem_limit_bytes=16 * 2**20),
        cost_estimate=pl.CostEstimate(
            flops=2 * rows * depth * columns,
            bytes_accessed=2 * depth * columns + 7 * rows * columns,
            transcendentals=0,
        ),
    )(core.reshape(1), x, w, more)


def exchange(x, axes):
    return lax.all_to_all(x, axes, split_axis=0, concat_axis=0, tiled=True)


def per_device(
    resid, query, new_kv, key_cache, value_cache, lengths, out_weight, hidden, down_weight
):
    gx, gyx, core = lax.axis_index("gx"), lax.axis_index("gyx"), lax.axis_index("core")

    pair = jnp.concatenate([key_cache, value_cache], -1)
    pair, own = lax.optimization_barrier((pair, hidden))
    pair = lax.ppermute(pair, "core", [(0, 1), (1, 0)])
    near = lax.ppermute(own, "gx", [(i, i ^ 1) for i in range(4)])
    keys = jnp.concatenate([key_cache, pair[..., :HD]], 1)
    values = jnp.concatenate([value_cache, pair[..., HD:]], 1)
    keys, near = lax.optimization_barrier((keys, near))
    near = jnp.where(gx % 2 == 0, jnp.stack([hidden, near]), jnp.stack([near, hidden]))
    far = lax.ppermute(near, "gx", [(i, i ^ 2) for i in range(4)])
    q = exchange(query.reshape(2, 16, 4, 768).transpose(1, 2, 0, 3), "gz")
    q = lax.dynamic_index_in_dim(q.reshape(4, 2, 2, 4, 2, 768), core, 1, keepdims=False)
    qf = q.reshape(4, 2, 4, 2, 3, HD).transpose(2, 0, 1, 3, 4, 5).reshape(4, 48, HD)

    at = jnp.arange(256, dtype=jnp.int32)
    owner = gx * 8 + gyx * 2 + jnp.where(at < 128, core, 1 - core)
    positions = owner * 128 + at % 128
    present = (positions[None] < lengths[:, None])[:, None]
    scale = HD**-0.5
    s = jnp.einsum("bqd,bpd->bqp", qf, keys, preferred_element_type=F32) * scale
    s = jnp.where(present, s, NEG)
    step = (jnp.arange(48) // 3) % 2
    allowed = (jnp.arange(2)[None, :] <= step[:, None]) & (gx + gyx == 0)
    sn = jnp.einsum("bqd,ubd->bqu", qf, new_kv[..., :HD], preferred_element_type=F32) * scale
    sn = jnp.where(allowed, sn, NEG)
    peak = jnp.maximum(jnp.max(s, -1), jnp.max(sn, -1)).astype(BF16)
    pf = peak.astype(F32)[..., None]
    w = jnp.where(present, jnp.exp(s - pf), 0.0).astype(BF16)
    wn = jnp.where(allowed, jnp.exp(sn - pf), 0.0).astype(BF16)
    total = jnp.sum(w.astype(F32), -1) + jnp.sum(wn.astype(F32), -1)
    acc = jnp.einsum("bqp,bpd->bqd", w, values, preferred_element_type=F32)
    acc = acc + jnp.einsum("bqu,ubd->bqd", wn, new_kv[..., HD:], preferred_element_type=F32)
    total_hi = total.astype(BF16)
    total_lo = (total - total_hi.astype(F32)).astype(BF16)
    stats = jnp.stack([peak, total_hi, total_lo, jnp.zeros_like(peak)], 1)
    stats = stats.reshape(4, 4, 4, 12).transpose(0, 2, 1, 3).reshape(16, 4, 12)
    stats = jnp.pad(stats, ((0, 0), (0, 0), (0, HD - 12)))
    message = jnp.concatenate([acc.astype(BF16).reshape(16, 12, HD), stats], 1)

    message = exchange(message, ("gx", "gyx"))
    peaks = message[:, 12, :12].astype(F32)
    totals = message[:, 13, :12].astype(F32) + message[:, 14, :12].astype(F32)
    share = jnp.exp(peaks - jnp.max(peaks, 0))
    share = share / jnp.sum(share * totals, 0)
    attn = jnp.sum(message[:, :12].astype(F32) * share[..., None], 0).astype(BF16)
    attn = attn.reshape(2, 2, 3, HD).transpose(1, 0, 2, 3).reshape(2, 16, 96).transpose(1, 0, 2)
    attn = jnp.broadcast_to(attn[:, None], (16, 4, 2, 96)).reshape(64, 2, 96)

    spread = jnp.where(gx < 2, jnp.concatenate([near, far]), jnp.concatenate([far, near]))
    feed = turned_product(spread.reshape(4, 32, 288), down_weight)

    mine = exchange(attn, ("gz", "gx")).transpose(1, 0, 2).reshape(128, 96)
    ours, theirs = split_product(core, mine, out_weight, feed)

    theirs = lax.ppermute(theirs, "core", [(0, 1), (1, 0)])
    row = (ours + theirs.astype(F32)).astype(BF16).reshape(4, 576, 128)
    row = exchange(row, "gyx")
    row = jnp.sum(row.astype(F32), 0).astype(BF16).reshape(16, 36, 128)
    column = exchange(row, "gz")
    summed = jnp.sum(column.astype(F32), 0).reshape(36, 2, 64).transpose(1, 2, 0)
    return (summed + resid.astype(F32)).astype(BF16)


def solution(mesh):
    mesh = Mesh(mesh.devices.reshape(4, 4, 2, 16), ("gx", "gyx", "core", "gz"))
    rows = GY + ("gz",)
    width = P(None, None, ("gx",) + rows)
    in_specs = (
        width,
        P(None, None, "gz"),
        P(None, "gz", None),
        P("gz", ("gx",) + GY, None),
        P("gz", ("gx",) + GY, None),
        P("gz"),
        P(rows, "gx"),
        P(None, "gx", rows),
        P(rows, "gx"),
    )
    return jax.shard_map(
        per_device, mesh=mesh, in_specs=in_specs, out_specs=width, check_vma=False
    )
```

```python
import jax
import jax.numpy as jnp
from jax import lax
from jax.experimental import pallas as pl
from jax.experimental.pallas import tpu as pltpu
from jax.sharding import Mesh
from jax.sharding import PartitionSpec as P

HEADS = 48
HD = 256
F32 = jnp.float32
BF16 = jnp.bfloat16
GY = ("gyx", "core")
NEG = -1e30
TILE = 1152


def turned_product(gathered, w):
    shares, held, width = gathered.shape
    rows = shares * held
    columns = w.shape[1]
    tiles = columns // TILE

    def kernel(h_ref, w_hbm, o_ref, w_buf, sems):
        copies = []
        for i in range(tiles):
            place = pl.ds(i * TILE, TILE)
            copies.append(pltpu.make_async_copy(w_hbm.at[:, place], w_buf.at[i], sems.at[i]))
            copies[-1].start()
        hidden = jnp.concatenate(
            [h_ref[s, 16 * t : 16 * t + 16, :] for t in range(2) for s in range(shares)], 0
        )
        for i in range(tiles):
            copies[i].wait()
            y = jnp.dot(hidden, w_buf[i], preferred_element_type=F32)
            o_ref[pl.ds(i * TILE, TILE), :] = y.T

    in_vmem = pl.BlockSpec(memory_space=pltpu.VMEM)
    return pl.pallas_call(
        kernel,
        in_specs=[in_vmem, pl.BlockSpec(memory_space=pltpu.HBM)],
        out_specs=in_vmem,
        out_shape=jax.ShapeDtypeStruct((columns, rows), F32),
        scratch_shapes=[
            pltpu.VMEM((tiles, width, TILE), BF16),
            pltpu.SemaphoreType.DMA((tiles,)),
        ],
        compiler_params=pltpu.CompilerParams(vmem_limit_bytes=51 * 2**20),
        cost_estimate=pl.CostEstimate(
            flops=2 * rows * width * columns,
            bytes_accessed=2 * width * columns + 4 * rows * columns,
            transcendentals=0,
        ),
    )(gathered, w)


def split_product(core, x, w, more):
    rows, depth = x.shape
    columns = w.shape[1]
    half = TILE // 2

    def kernel(core_ref, x_ref, w_ref, more_ref, ours_ref, theirs_ref, full):
        mine = core_ref[0]
        for i in range(columns // TILE):
            place = pl.ds(i * TILE, TILE)
            y = jnp.dot(x_ref[...], w_ref[:, place], preferred_element_type=F32)
            full[...] = y.T + more_ref[place, :]
            rows_i = pl.ds(i * half, half)
            ours_ref[rows_i, :] = full[pl.ds(pl.multiple_of(mine * half, half), half), :]
            theirs = full[pl.ds(pl.multiple_of((1 - mine) * half, half), half), :]
            theirs_ref[rows_i, :] = theirs.astype(BF16)

    in_vmem = pl.BlockSpec(memory_space=pltpu.VMEM)
    return pl.pallas_call(
        kernel,
        in_specs=[pl.BlockSpec(memory_space=pltpu.SMEM), in_vmem, in_vmem, in_vmem],
        out_specs=[in_vmem, in_vmem],
        out_shape=[
            jax.ShapeDtypeStruct((columns // 2, rows), F32),
            jax.ShapeDtypeStruct((columns // 2, rows), BF16),
        ],
        scratch_shapes=[pltpu.VMEM((TILE, rows), F32)],
        compiler_params=pltpu.CompilerParams(vmem_limit_bytes=16 * 2**20),
        cost_estimate=pl.CostEstimate(
            flops=2 * rows * depth * columns,
            bytes_accessed=2 * depth * columns + 7 * rows * columns,
            transcendentals=0,
        ),
    )(core.reshape(1), x, w, more)


def exchange(x, axes):
    return lax.all_to_all(x, axes, split_axis=0, concat_axis=0, tiled=True)


def per_device(
    resid, query, new_kv, key_cache, value_cache, lengths, out_weight, hidden, down_weight
):
    gx, gyx, core = lax.axis_index("gx"), lax.axis_index("gyx"), lax.axis_index("core")

    pair = jnp.concatenate([key_cache, value_cache], -1)
    pair, own = lax.optimization_barrier((pair, hidden))
    pair = lax.ppermute(pair, "core", [(0, 1), (1, 0)])
    near = lax.ppermute(own, "gx", [(i, i ^ 1) for i in range(4)])
    keys = jnp.concatenate([key_cache, pair[..., :HD]], 1)
    values = jnp.concatenate([value_cache, pair[..., HD:]], 1)
    keys, near = lax.optimization_barrier((keys, near))
    near = jnp.where(gx % 2 == 0, jnp.stack([hidden, near]), jnp.stack([near, hidden]))
    far = lax.ppermute(near, "gx", [(i, i ^ 2) for i in range(4)])
    q = lax.dynamic_index_in_dim(query, core, 0, keepdims=False)
    q = exchange(q.reshape(16, 4, 768), "gz")
    qf = q.reshape(16, 4, 3, HD).transpose(1, 0, 2, 3).reshape(4, HEADS, HD)

    at = jnp.arange(256, dtype=jnp.int32)
    owner = gx * 8 + gyx * 2 + jnp.where(at < 128, core, 1 - core)
    positions = owner * 128 + at % 128
    present = (positions[None] < lengths[:, None])[:, None]
    scale = HD**-0.5
    s = jnp.einsum("bqd,bpd->bqp", qf, keys, preferred_element_type=F32) * scale
    s = jnp.where(present, s, NEG)
    allowed = ((jnp.arange(2) <= core) & (gx + gyx == 0))[None, None]
    sn = jnp.einsum("bqd,ubd->bqu", qf, new_kv[..., :HD], preferred_element_type=F32) * scale
    sn = jnp.where(allowed, sn, NEG)
    peak = jnp.maximum(jnp.max(s, -1), jnp.max(sn, -1)).astype(BF16)
    pf = peak.astype(F32)[..., None]
    w = jnp.where(present, jnp.exp(s - pf), 0.0).astype(BF16)
    wn = jnp.where(allowed, jnp.exp(sn - pf), 0.0).astype(BF16)
    total = jnp.sum(w.astype(F32), -1) + jnp.sum(wn.astype(F32), -1)
    acc = jnp.einsum("bqp,bpd->bqd", w, values, preferred_element_type=F32)
    acc = acc + jnp.einsum("bqu,ubd->bqd", wn, new_kv[..., HD:], preferred_element_type=F32)
    total_hi = total.astype(BF16)
    total_lo = (total - total_hi.astype(F32)).astype(BF16)
    stats = jnp.stack([peak, total_hi, total_lo, jnp.zeros_like(peak)], 1)
    stats = stats.reshape(4, 4, 4, 12).transpose(0, 2, 1, 3).reshape(16, 4, 12)
    stats = jnp.pad(stats, ((0, 0), (0, 0), (0, HD - 12)))
    message = jnp.concatenate([acc.astype(BF16).reshape(16, 12, HD), stats], 1)

    message = exchange(message, ("gx", "gyx"))
    peaks = message[:, 12, :12].astype(F32)
    totals = message[:, 13, :12].astype(F32) + message[:, 14, :12].astype(F32)
    share = jnp.exp(peaks - jnp.max(peaks, 0))
    share = share / jnp.sum(share * totals, 0)
    attn = jnp.sum(message[:, :12].astype(F32) * share[..., None], 0).astype(BF16)
    attn = attn.reshape(2, 16, 96).transpose(1, 0, 2)
    attn = jnp.broadcast_to(attn[:, None], (16, 4, 2, 96)).reshape(128, 1, 96)

    spread = jnp.where(gx < 2, jnp.concatenate([near, far]), jnp.concatenate([far, near]))
    feed = turned_product(spread.reshape(4, 32, 288), down_weight)

    mine = exchange(attn, ("gz", "gx", "core"))
    mine = mine.reshape(64, 2, 96).transpose(1, 0, 2).reshape(128, 96)
    ours, theirs = split_product(core, mine, out_weight, feed)

    theirs = lax.ppermute(theirs, "core", [(0, 1), (1, 0)])
    row = (ours + theirs.astype(F32)).astype(BF16).reshape(4, 576, 128)
    row = exchange(row, "gyx")
    row = jnp.sum(row.astype(F32), 0).astype(BF16).reshape(16, 36, 128)
    column = exchange(row, "gz")
    summed = jnp.sum(column.astype(F32), 0).reshape(36, 2, 64).transpose(1, 2, 0)
    return (summed + resid.astype(F32)).astype(BF16)


def solution(mesh):
    mesh = Mesh(mesh.devices.reshape(4, 4, 2, 16), ("gx", "gyx", "core", "gz"))
    rows = GY + ("gz",)
    width = P(None, None, ("gx",) + rows)
    in_specs = (
        width,
        P(None, None, "gz"),
        P(None, "gz", None),
        P("gz", ("gx",) + GY, None),
        P("gz", ("gx",) + GY, None),
        P("gz"),
        P(rows, "gx"),
        P(None, "gx", rows),
        P(rows, "gx"),
    )
    return jax.shard_map(
        per_device, mesh=mesh, in_specs=in_specs, out_specs=width, check_vma=False
    )
```

```python
import jax
import jax.numpy as jnp
from jax import lax
from jax.experimental import pallas as pl
from jax.experimental.pallas import tpu as pltpu
from jax.sharding import Mesh
from jax.sharding import PartitionSpec as P

HEADS = 48
HD = 256
F32 = jnp.float32
BF16 = jnp.bfloat16
GY = ("gyx", "core")
NEG = -1e30
TILE = 1152


def turned_product(gathered, w):
    shares, held, width = gathered.shape
    rows = shares * held
    columns = w.shape[1]
    tiles = columns // TILE

    def kernel(h_ref, w_hbm, o_ref, w_buf, sems):
        copies = []
        for i in range(tiles):
            place = pl.ds(i * TILE, TILE)
            copies.append(pltpu.make_async_copy(w_hbm.at[:, place], w_buf.at[i], sems.at[i]))
            copies[-1].start()
        hidden = jnp.concatenate(
            [h_ref[s, 16 * t : 16 * t + 16, :] for t in range(2) for s in range(shares)], 0
        )
        for i in range(tiles):
            copies[i].wait()
            y = jnp.dot(hidden, w_buf[i], preferred_element_type=F32)
            o_ref[pl.ds(i * TILE, TILE), :] = y.T

    in_vmem = pl.BlockSpec(memory_space=pltpu.VMEM)
    return pl.pallas_call(
        kernel,
        in_specs=[in_vmem, pl.BlockSpec(memory_space=pltpu.HBM)],
        out_specs=in_vmem,
        out_shape=jax.ShapeDtypeStruct((columns, rows), F32),
        scratch_shapes=[
            pltpu.VMEM((tiles, width, TILE), BF16),
            pltpu.SemaphoreType.DMA((tiles,)),
        ],
        compiler_params=pltpu.CompilerParams(vmem_limit_bytes=51 * 2**20),
        cost_estimate=pl.CostEstimate(
            flops=2 * rows * width * columns,
            bytes_accessed=2 * width * columns + 4 * rows * columns,
            transcendentals=0,
        ),
    )(gathered, w)


def split_product(core, x, w, more):
    rows, depth = x.shape
    columns = w.shape[1]
    half = TILE // 2

    def kernel(core_ref, x_ref, w_ref, more_ref, ours_ref, theirs_ref, full):
        mine = core_ref[0]
        for i in range(columns // TILE):
            place = pl.ds(i * TILE, TILE)
            y = jnp.dot(x_ref[...], w_ref[:, place], preferred_element_type=F32)
            full[...] = y.T + more_ref[place, :]
            rows_i = pl.ds(i * half, half)
            ours_ref[rows_i, :] = full[pl.ds(pl.multiple_of(mine * half, half), half), :]
            theirs = full[pl.ds(pl.multiple_of((1 - mine) * half, half), half), :]
            theirs_ref[rows_i, :] = theirs.astype(BF16)

    in_vmem = pl.BlockSpec(memory_space=pltpu.VMEM)
    return pl.pallas_call(
        kernel,
        in_specs=[pl.BlockSpec(memory_space=pltpu.SMEM), in_vmem, in_vmem, in_vmem],
        out_specs=[in_vmem, in_vmem],
        out_shape=[
            jax.ShapeDtypeStruct((columns // 2, rows), F32),
            jax.ShapeDtypeStruct((columns // 2, rows), BF16),
        ],
        scratch_shapes=[pltpu.VMEM((TILE, rows), F32)],
        compiler_params=pltpu.CompilerParams(vmem_limit_bytes=16 * 2**20),
        cost_estimate=pl.CostEstimate(
            flops=2 * rows * depth * columns,
            bytes_accessed=2 * depth * columns + 7 * rows * columns,
            transcendentals=0,
        ),
    )(core.reshape(1), x, w, more)


def exchange(x, axes):
    return lax.all_to_all(x, axes, split_axis=0, concat_axis=0, tiled=True)


def per_device(
    resid, query, new_kv, key_cache, value_cache, lengths, out_weight, hidden, down_weight
):
    gx, gyx, core = lax.axis_index("gx"), lax.axis_index("gyx"), lax.axis_index("core")

    pair = jnp.concatenate([key_cache, value_cache], -1)
    pair, own = lax.optimization_barrier((pair, hidden))
    pair = lax.ppermute(pair, "core", [(0, 1), (1, 0)])
    near = lax.ppermute(own, "gx", [(i, i ^ 1) for i in range(4)])
    keys = jnp.concatenate([key_cache, pair[..., :HD]], 1)
    values = jnp.concatenate([value_cache, pair[..., HD:]], 1)
    near = jnp.where(gx % 2 == 0, jnp.stack([hidden, near]), jnp.stack([near, hidden]))
    far = lax.ppermute(near, "gx", [(i, i ^ 2) for i in range(4)])
    spread = jnp.where(gx < 2, jnp.concatenate([near, far]), jnp.concatenate([far, near]))
    keys, spread = lax.optimization_barrier((keys, spread))
    q = lax.dynamic_index_in_dim(query, core, 0, keepdims=False)
    q = exchange(q.reshape(16, 4, 768), "gz")
    qf = q.reshape(16, 4, 3, HD).transpose(1, 0, 2, 3).reshape(4, HEADS, HD)

    at = jnp.arange(256, dtype=jnp.int32)
    owner = gx * 8 + gyx * 2 + jnp.where(at < 128, core, 1 - core)
    positions = owner * 128 + at % 128
    present = (positions[None] < lengths[:, None])[:, None]
    scale = HD**-0.5
    s = jnp.einsum("bqd,bpd->bqp", qf, keys, preferred_element_type=F32) * scale
    s = jnp.where(present, s, NEG)
    allowed = ((jnp.arange(2) <= core) & (gx + gyx == 0))[None, None]
    sn = jnp.einsum("bqd,ubd->bqu", qf, new_kv[..., :HD], preferred_element_type=F32) * scale
    sn = jnp.where(allowed, sn, NEG)
    peak = jnp.maximum(jnp.max(s, -1), jnp.max(sn, -1)).astype(BF16)
    pf = peak.astype(F32)[..., None]
    w = jnp.where(present, jnp.exp(s - pf), 0.0).astype(BF16)
    wn = jnp.where(allowed, jnp.exp(sn - pf), 0.0).astype(BF16)
    total = jnp.sum(w.astype(F32), -1) + jnp.sum(wn.astype(F32), -1)
    acc = jnp.einsum("bqp,bpd->bqd", w, values, preferred_element_type=F32)
    acc = acc + jnp.einsum("bqu,ubd->bqd", wn, new_kv[..., HD:], preferred_element_type=F32)
    total_hi = total.astype(BF16)
    total_lo = (total - total_hi.astype(F32)).astype(BF16)
    stats = jnp.stack([peak, total_hi, total_lo], 1)
    stats = stats.reshape(4, 3, 8, 6).transpose(0, 2, 1, 3).reshape(32, 1, 18)
    stats = jnp.pad(stats, ((0, 0), (0, 1), (0, HD - 18)))
    message = jnp.concatenate([acc.astype(BF16).reshape(32, 6, HD), stats], 1)

    message = exchange(message, ("gx",) + GY).reshape(16, 2, 8, HD)
    peaks = message[:, :, 6, :6].astype(F32)
    totals = message[:, :, 6, 6:12].astype(F32) + message[:, :, 6, 12:18].astype(F32)
    share = jnp.exp(peaks - jnp.max(peaks, 0))
    share = share / jnp.sum(share * totals, 0)
    attn = jnp.sum(message[:, :, :6].astype(F32) * share[..., None], 0).astype(BF16)
    attn = attn.reshape(2, 16, 96).transpose(1, 0, 2)
    attn = jnp.broadcast_to(attn[:, None], (16, 4, 2, 96)).reshape(64, 2, 96)
    feed = turned_product(spread.reshape(4, 32, 288), down_weight)

    mine = exchange(attn, ("gz", "gx")).transpose(1, 0, 2).reshape(128, 96)
    ours, theirs = split_product(core, mine, out_weight, feed)

    theirs = lax.ppermute(theirs, "core", [(0, 1), (1, 0)])
    row = (ours + theirs.astype(F32)).astype(BF16).reshape(4, 576, 128)
    row = exchange(row, "gyx")
    row = jnp.sum(row.astype(F32), 0).astype(BF16).reshape(16, 9, 4, 128)
    column = exchange(row, "gz").reshape(16, 36, 128)
    summed = jnp.sum(column.astype(F32), 0).reshape(36, 2, 64).transpose(1, 2, 0)
    return (summed + resid.astype(F32)).astype(BF16)


def solution(mesh):
    mesh = Mesh(mesh.devices.reshape(4, 4, 2, 16), ("gx", "gyx", "core", "gz"))
    rows = GY + ("gz",)
    width = P(None, None, ("gx",) + rows)
    in_specs = (
        width,
        P(None, None, "gz"),
        P(None, "gz", None),
        P("gz", ("gx",) + GY, None),
        P("gz", ("gx",) + GY, None),
        P("gz"),
        P(rows, "gx"),
        P(None, "gx", rows),
        P(rows, "gx"),
    )
    return jax.shard_map(
        per_device, mesh=mesh, in_specs=in_specs, out_specs=width, check_vma=False
    )
```

```python
import jax
import jax.numpy as jnp
from jax import lax
from jax.experimental import pallas as pl
from jax.experimental.pallas import tpu as pltpu
from jax.sharding import Mesh
from jax.sharding import PartitionSpec as P

HEADS = 48
HD = 256
F32 = jnp.float32
BF16 = jnp.bfloat16
GY = ("gyx", "core")
NEG = -1e30
TILE = 1152


def turned_product(gathered, w):
    shares, held, width = gathered.shape
    rows = shares * held
    columns = w.shape[1]
    tiles = columns // TILE

    def kernel(h_ref, w_hbm, o_ref, w_buf, sems):
        copies = []
        for i in range(tiles):
            place = pl.ds(i * TILE, TILE)
            copies.append(pltpu.make_async_copy(w_hbm.at[:, place], w_buf.at[i], sems.at[i]))
            copies[-1].start()
        hidden = jnp.concatenate(
            [h_ref[s, 16 * t : 16 * t + 16, :] for t in range(2) for s in range(shares)], 0
        )
        for i in range(tiles):
            copies[i].wait()
            y = jnp.dot(hidden, w_buf[i], preferred_element_type=F32)
            o_ref[pl.ds(i * TILE, TILE), :] = y.T

    in_vmem = pl.BlockSpec(memory_space=pltpu.VMEM)
    return pl.pallas_call(
        kernel,
        in_specs=[in_vmem, pl.BlockSpec(memory_space=pltpu.HBM)],
        out_specs=in_vmem,
        out_shape=jax.ShapeDtypeStruct((columns, rows), F32),
        scratch_shapes=[
            pltpu.VMEM((tiles, width, TILE), BF16),
            pltpu.SemaphoreType.DMA((tiles,)),
        ],
        compiler_params=pltpu.CompilerParams(vmem_limit_bytes=51 * 2**20),
        cost_estimate=pl.CostEstimate(
            flops=2 * rows * width * columns,
            bytes_accessed=2 * width * columns + 4 * rows * columns,
            transcendentals=0,
        ),
    )(gathered, w)


def split_product(core, x, w, more):
    rows, depth = x.shape
    columns = w.shape[1]
    half = TILE // 2

    def kernel(core_ref, x_ref, w_ref, more_ref, ours_ref, theirs_ref, full):
        mine = core_ref[0]
        for i in range(columns // TILE):
            place = pl.ds(i * TILE, TILE)
            y = jnp.dot(x_ref[...], w_ref[:, place], preferred_element_type=F32)
            full[...] = y.T + more_ref[place, :]
            rows_i = pl.ds(i * half, half)
            ours_ref[rows_i, :] = full[pl.ds(pl.multiple_of(mine * half, half), half), :]
            theirs = full[pl.ds(pl.multiple_of((1 - mine) * half, half), half), :]
            theirs_ref[rows_i, :] = theirs.astype(BF16)

    in_vmem = pl.BlockSpec(memory_space=pltpu.VMEM)
    return pl.pallas_call(
        kernel,
        in_specs=[pl.BlockSpec(memory_space=pltpu.SMEM), in_vmem, in_vmem, in_vmem],
        out_specs=[in_vmem, in_vmem],
        out_shape=[
            jax.ShapeDtypeStruct((columns // 2, rows), F32),
            jax.ShapeDtypeStruct((columns // 2, rows), BF16),
        ],
        scratch_shapes=[pltpu.VMEM((TILE, rows), F32)],
        compiler_params=pltpu.CompilerParams(vmem_limit_bytes=16 * 2**20),
        cost_estimate=pl.CostEstimate(
            flops=2 * rows * depth * columns,
            bytes_accessed=2 * depth * columns + 7 * rows * columns,
            transcendentals=0,
        ),
    )(core.reshape(1), x, w, more)


def exchange(x, axes):
    return lax.all_to_all(x, axes, split_axis=0, concat_axis=0, tiled=True)


def per_device(
    resid, query, new_kv, key_cache, value_cache, lengths, out_weight, hidden, down_weight
):
    gx, gyx, core = lax.axis_index("gx"), lax.axis_index("gyx"), lax.axis_index("core")

    pair = jnp.concatenate([key_cache, value_cache], -1)
    pair, own = lax.optimization_barrier((pair, hidden))
    pair = lax.ppermute(pair, "core", [(0, 1), (1, 0)])
    near = lax.ppermute(own, "gx", [(i, i ^ 1) for i in range(4)])
    keys = jnp.concatenate([key_cache, pair[..., :HD]], 1)
    values = jnp.concatenate([value_cache, pair[..., HD:]], 1)
    near = jnp.where(gx % 2 == 0, jnp.stack([hidden, near]), jnp.stack([near, hidden]))
    keys, near = lax.optimization_barrier((keys, near))
    q = exchange(query.reshape(2, 16, 4, 768).transpose(1, 2, 0, 3), "gz")
    q = lax.dynamic_index_in_dim(q.reshape(4, 2, 2, 4, 2, 768), core, 1, keepdims=False)
    qf = q.reshape(4, 2, 4, 2, 3, HD).transpose(2, 0, 1, 3, 4, 5).reshape(4, 48, HD)

    at = jnp.arange(256, dtype=jnp.int32)
    owner = gx * 8 + gyx * 2 + jnp.where(at < 128, core, 1 - core)
    positions = owner * 128 + at % 128
    present = (positions[None] < lengths[:, None])[:, None]
    scale = HD**-0.5
    s = jnp.einsum("bqd,bpd->bqp", qf, keys, preferred_element_type=F32) * scale
    s = jnp.where(present, s, NEG)
    step = (jnp.arange(48) // 3) % 2
    allowed = (jnp.arange(2)[None, :] <= step[:, None]) & (gx + gyx == 0)
    sn = jnp.einsum("bqd,ubd->bqu", qf, new_kv[..., :HD], preferred_element_type=F32) * scale
    sn = jnp.where(allowed, sn, NEG)
    peak = jnp.maximum(jnp.max(s, -1), jnp.max(sn, -1)).astype(BF16)
    pf = peak.astype(F32)[..., None]
    w = jnp.where(present, jnp.exp(s - pf), 0.0).astype(BF16)
    wn = jnp.where(allowed, jnp.exp(sn - pf), 0.0).astype(BF16)
    total = jnp.sum(w.astype(F32), -1) + jnp.sum(wn.astype(F32), -1)
    acc = jnp.einsum("bqp,bpd->bqd", w, values, preferred_element_type=F32)
    acc = acc + jnp.einsum("bqu,ubd->bqd", wn, new_kv[..., HD:], preferred_element_type=F32)
    total_hi = total.astype(BF16)
    total_lo = (total - total_hi.astype(F32)).astype(BF16)
    stats = jnp.stack([peak, total_hi, total_lo, jnp.zeros_like(peak)], 1)
    stats = stats.reshape(4, 4, 4, 12).transpose(0, 2, 1, 3).reshape(16, 4, 12)
    stats = jnp.pad(stats, ((0, 0), (0, 0), (0, HD - 12)))
    message = jnp.concatenate([acc.astype(BF16).reshape(16, 12, HD), stats], 1)

    message = exchange(message, ("gx", "gyx"))
    peaks = message[:, 12, :12].astype(F32)
    totals = message[:, 13, :12].astype(F32) + message[:, 14, :12].astype(F32)
    share = jnp.exp(peaks - jnp.max(peaks, 0))
    share = share / jnp.sum(share * totals, 0)
    attn = jnp.sum(message[:, :12].astype(F32) * share[..., None], 0).astype(BF16)
    attn = attn.reshape(2, 2, 3, HD).transpose(1, 0, 2, 3).reshape(2, 16, 96).transpose(1, 0, 2)
    attn = jnp.broadcast_to(attn[:, None], (16, 4, 2, 96)).reshape(64, 2, 96)

    attn, near = lax.optimization_barrier((attn, near))
    far = lax.ppermute(near, "gx", [(i, i ^ 2) for i in range(4)])
    spread = jnp.where(gx < 2, jnp.concatenate([near, far]), jnp.concatenate([far, near]))
    feed = turned_product(spread.reshape(4, 32, 288), down_weight)

    attn = jnp.pad(attn, ((0, 0), (0, 0), (0, 160)))
    mine = exchange(attn, ("gz", "gx"))[..., :96].transpose(1, 0, 2).reshape(128, 96)
    ours, theirs = split_product(core, mine, out_weight, feed)

    theirs = lax.ppermute(theirs, "core", [(0, 1), (1, 0)])
    row = (ours + theirs.astype(F32)).astype(BF16).reshape(4, 576, 128)
    row = exchange(row, "gyx")
    row = jnp.sum(row.astype(F32), 0).astype(BF16).reshape(16, 9, 4, 128)
    column = exchange(row, "gz").reshape(16, 36, 128)
    summed = jnp.sum(column.astype(F32), 0).reshape(36, 2, 64).transpose(1, 2, 0)
    return (summed + resid.astype(F32)).astype(BF16)


def solution(mesh):
    mesh = Mesh(mesh.devices.reshape(4, 4, 2, 16), ("gx", "gyx", "core", "gz"))
    rows = GY + ("gz",)
    width = P(None, None, ("gx",) + rows)
    in_specs = (
        width,
        P(None, None, "gz"),
        P(None, "gz", None),
        P("gz", ("gx",) + GY, None),
        P("gz", ("gx",) + GY, None),
        P("gz"),
        P(rows, "gx"),
        P(None, "gx", rows),
        P(rows, "gx"),
    )
    return jax.shard_map(
        per_device, mesh=mesh, in_specs=in_specs, out_specs=width, check_vma=False
    )
```

```python
import jax
import jax.numpy as jnp
from jax import lax
from jax.experimental import pallas as pl
from jax.experimental.pallas import tpu as pltpu
from jax.sharding import Mesh
from jax.sharding import PartitionSpec as P

HEADS = 48
HD = 256
F32 = jnp.float32
BF16 = jnp.bfloat16
GY = ("gyx", "core")
NEG = -1e30
TILE = 1152


def turned_product(gathered, w):
    shares, held, width = gathered.shape
    rows = shares * held
    columns = w.shape[1]
    tiles = columns // TILE

    def kernel(h_ref, w_hbm, o_ref, w_buf, sems):
        copies = []
        for i in range(tiles):
            place = pl.ds(i * TILE, TILE)
            copies.append(pltpu.make_async_copy(w_hbm.at[:, place], w_buf.at[i], sems.at[i]))
            copies[-1].start()
        hidden = jnp.concatenate(
            [h_ref[s, 16 * t : 16 * t + 16, :] for t in range(2) for s in range(shares)], 0
        )
        for i in range(tiles):
            copies[i].wait()
            y = jnp.dot(hidden, w_buf[i], preferred_element_type=F32)
            o_ref[pl.ds(i * TILE, TILE), :] = y.T

    in_vmem = pl.BlockSpec(memory_space=pltpu.VMEM)
    return pl.pallas_call(
        kernel,
        in_specs=[in_vmem, pl.BlockSpec(memory_space=pltpu.HBM)],
        out_specs=in_vmem,
        out_shape=jax.ShapeDtypeStruct((columns, rows), F32),
        scratch_shapes=[
            pltpu.VMEM((tiles, width, TILE), BF16),
            pltpu.SemaphoreType.DMA((tiles,)),
        ],
        compiler_params=pltpu.CompilerParams(vmem_limit_bytes=51 * 2**20),
        cost_estimate=pl.CostEstimate(
            flops=2 * rows * width * columns,
            bytes_accessed=2 * width * columns + 4 * rows * columns,
            transcendentals=0,
        ),
    )(gathered, w)


def split_product(core, x, w, more):
    rows, depth = x.shape
    columns = w.shape[1]
    half = TILE // 2

    def kernel(core_ref, x_ref, w_ref, more_ref, ours_ref, theirs_ref, full):
        mine = core_ref[0]
        for i in range(columns // TILE):
            place = pl.ds(i * TILE, TILE)
            y = jnp.dot(x_ref[...], w_ref[:, place], preferred_element_type=F32)
            full[...] = y.T + more_ref[place, :]
            rows_i = pl.ds(i * half, half)
            ours_ref[rows_i, :] = full[pl.ds(pl.multiple_of(mine * half, half), half), :]
            theirs = full[pl.ds(pl.multiple_of((1 - mine) * half, half), half), :]
            theirs_ref[rows_i, :] = theirs.astype(BF16)

    in_vmem = pl.BlockSpec(memory_space=pltpu.VMEM)
    return pl.pallas_call(
        kernel,
        in_specs=[pl.BlockSpec(memory_space=pltpu.SMEM), in_vmem, in_vmem, in_vmem],
        out_specs=[in_vmem, in_vmem],
        out_shape=[
            jax.ShapeDtypeStruct((columns // 2, rows), F32),
            jax.ShapeDtypeStruct((columns // 2, rows), BF16),
        ],
        scratch_shapes=[pltpu.VMEM((TILE, rows), F32)],
        compiler_params=pltpu.CompilerParams(vmem_limit_bytes=16 * 2**20),
        cost_estimate=pl.CostEstimate(
            flops=2 * rows * depth * columns,
            bytes_accessed=2 * depth * columns + 7 * rows * columns,
            transcendentals=0,
        ),
    )(core.reshape(1), x, w, more)


def exchange(x, axes):
    return lax.all_to_all(x, axes, split_axis=0, concat_axis=0, tiled=True)


def per_device(
    resid, query, new_kv, key_cache, value_cache, lengths, out_weight, hidden, down_weight
):
    gx, gyx, core = lax.axis_index("gx"), lax.axis_index("gyx"), lax.axis_index("core")

    pair = jnp.concatenate([key_cache, value_cache], -1)
    pair, own = lax.optimization_barrier((pair, hidden))
    pair = lax.ppermute(pair, "core", [(0, 1), (1, 0)])
    near = lax.ppermute(own, "gx", [(i, i ^ 1) for i in range(4)])
    keys = jnp.concatenate([key_cache, pair[..., :HD]], 1)
    values = jnp.concatenate([value_cache, pair[..., HD:]], 1)
    keys, near = lax.optimization_barrier((keys, near))
    near = jnp.where(gx % 2 == 0, jnp.stack([hidden, near]), jnp.stack([near, hidden]))
    far = lax.ppermute(near, "gx", [(i, i ^ 2) for i in range(4)])
    q = lax.dynamic_index_in_dim(query, core, 0, keepdims=False)
    q = exchange(q.reshape(16, 4, 768), "gz")
    qf = q.reshape(16, 4, 3, HD).transpose(1, 0, 2, 3).reshape(4, HEADS, HD)

    at = jnp.arange(256, dtype=jnp.int32)
    owner = gx * 8 + gyx * 2 + jnp.where(at < 128, core, 1 - core)
    positions = owner * 128 + at % 128
    present = (positions[None] < lengths[:, None])[:, None]
    scale = HD**-0.5
    s = jnp.einsum("bqd,bpd->bqp", qf, keys, preferred_element_type=F32) * scale
    s = jnp.where(present, s, NEG)
    allowed = ((jnp.arange(2) <= core) & (gx + gyx == 0))[None, None]
    sn = jnp.einsum("bqd,ubd->bqu", qf, new_kv[..., :HD], preferred_element_type=F32) * scale
    sn = jnp.where(allowed, sn, NEG)
    peak = jnp.maximum(jnp.max(s, -1), jnp.max(sn, -1)).astype(BF16)
    pf = peak.astype(F32)[..., None]
    w = jnp.where(present, jnp.exp(s - pf), 0.0).astype(BF16)
    wn = jnp.where(allowed, jnp.exp(sn - pf), 0.0).astype(BF16)
    total = jnp.sum(w.astype(F32), -1) + jnp.sum(wn.astype(F32), -1)
    acc = jnp.einsum("bqp,bpd->bqd", w, values, preferred_element_type=F32)
    acc = acc + jnp.einsum("bqu,ubd->bqd", wn, new_kv[..., HD:], preferred_element_type=F32)
    total_hi = total.astype(BF16)
    total_lo = (total - total_hi.astype(F32)).astype(BF16)
    stats = jnp.stack([peak, total_hi, total_lo, jnp.zeros_like(peak)], 1)
    stats = stats.reshape(4, 4, 4, 12).transpose(0, 2, 1, 3).reshape(16, 4, 12)
    stats = jnp.pad(stats, ((0, 0), (0, 0), (0, HD - 12)))
    message = jnp.concatenate([acc.astype(BF16).reshape(16, 12, HD), stats], 1)

    message = exchange(message, ("gx", "gyx"))
    peaks = message[:, 12, :12].astype(F32)
    totals = message[:, 13, :12].astype(F32) + message[:, 14, :12].astype(F32)
    share = jnp.exp(peaks - jnp.max(peaks, 0))
    share = share / jnp.sum(share * totals, 0)
    attn = jnp.sum(message[:, :12].astype(F32) * share[..., None], 0).astype(BF16)
    attn = attn.reshape(2, 16, 96).transpose(1, 0, 2)
    attn = jnp.broadcast_to(attn[:, None], (16, 4, 2, 96)).reshape(128, 1, 96)

    spread = jnp.where(gx < 2, jnp.concatenate([near, far]), jnp.concatenate([far, near]))
    feed = turned_product(spread.reshape(4, 32, 288), down_weight)

    mine = exchange(attn, ("gz", "gx", "core"))
    mine = mine.reshape(64, 2, 96).transpose(1, 0, 2).reshape(128, 96)
    ours, theirs = split_product(core, mine, out_weight, feed)

    theirs = lax.ppermute(theirs, "core", [(0, 1), (1, 0)])
    row = (ours + theirs.astype(F32)).astype(BF16).reshape(4, 576, 128)
    row = exchange(row, "gyx")
    row = jnp.sum(row.astype(F32), 0).astype(BF16).reshape(16, 9, 4, 128)
    column = exchange(row, "gz").reshape(16, 36, 128)
    summed = jnp.sum(column.astype(F32), 0).reshape(36, 2, 64).transpose(1, 2, 0)
    return (summed + resid.astype(F32)).astype(BF16)


def solution(mesh):
    mesh = Mesh(mesh.devices.reshape(4, 4, 2, 16), ("gx", "gyx", "core", "gz"))
    rows = GY + ("gz",)
    width = P(None, None, ("gx",) + rows)
    in_specs = (
        width,
        P(None, None, "gz"),
        P(None, "gz", None),
        P("gz", ("gx",) + GY, None),
        P("gz", ("gx",) + GY, None),
        P("gz"),
        P(rows, "gx"),
        P(None, "gx", rows),
        P(rows, "gx"),
    )
    return jax.shard_map(
        per_device, mesh=mesh, in_specs=in_specs, out_specs=width, check_vma=False
    )
```

```python
import jax
import jax.numpy as jnp
from jax import lax
from jax.experimental import pallas as pl
from jax.experimental.pallas import tpu as pltpu
from jax.sharding import Mesh
from jax.sharding import PartitionSpec as P

HEADS = 48
HD = 256
F32 = jnp.float32
BF16 = jnp.bfloat16
GX = ("gxh", "gxl")
GY = ("gyx", "core")
NEG = -1e30
TILE = 1152


def turned_product(gathered, w):
    shares, held, width = gathered.shape
    rows = shares * held
    columns = w.shape[1]
    tiles = columns // TILE

    def kernel(h_ref, w_hbm, o_ref, w_buf, sems):
        copies = []
        for i in range(tiles):
            place = pl.ds(i * TILE, TILE)
            copies.append(pltpu.make_async_copy(w_hbm.at[:, place], w_buf.at[i], sems.at[i]))
            copies[-1].start()
        hidden = jnp.concatenate(
            [h_ref[s, 16 * t : 16 * t + 16, :] for t in range(2) for s in range(shares)], 0
        )
        for i in range(tiles):
            copies[i].wait()
            y = jnp.dot(hidden, w_buf[i], preferred_element_type=F32)
            o_ref[pl.ds(i * TILE, TILE), :] = y.T

    in_vmem = pl.BlockSpec(memory_space=pltpu.VMEM)
    return pl.pallas_call(
        kernel,
        in_specs=[in_vmem, pl.BlockSpec(memory_space=pltpu.HBM)],
        out_specs=in_vmem,
        out_shape=jax.ShapeDtypeStruct((columns, rows), F32),
        scratch_shapes=[
            pltpu.VMEM((tiles, width, TILE), BF16),
            pltpu.SemaphoreType.DMA((tiles,)),
        ],
        compiler_params=pltpu.CompilerParams(vmem_limit_bytes=51 * 2**20),
        cost_estimate=pl.CostEstimate(
            flops=2 * rows * width * columns,
            bytes_accessed=2 * width * columns + 4 * rows * columns,
            transcendentals=0,
        ),
    )(gathered, w)


def split_product(core, x, w, more):
    rows, depth = x.shape
    columns = w.shape[1]
    half = TILE // 2

    def kernel(core_ref, x_ref, w_ref, more_ref, ours_ref, theirs_ref, full):
        mine = core_ref[0]
        for i in range(columns // TILE):
            place = pl.ds(i * TILE, TILE)
            y = jnp.dot(x_ref[...], w_ref[:, place], preferred_element_type=F32)
            full[...] = y.T + more_ref[place, :]
            rows_i = pl.ds(i * half, half)
            ours_ref[rows_i, :] = full[pl.ds(pl.multiple_of(mine * half, half), half), :]
            theirs = full[pl.ds(pl.multiple_of((1 - mine) * half, half), half), :]
            theirs_ref[rows_i, :] = theirs.astype(BF16)

    in_vmem = pl.BlockSpec(memory_space=pltpu.VMEM)
    return pl.pallas_call(
        kernel,
        in_specs=[pl.BlockSpec(memory_space=pltpu.SMEM), in_vmem, in_vmem, in_vmem],
        out_specs=[in_vmem, in_vmem],
        out_shape=[
            jax.ShapeDtypeStruct((columns // 2, rows), F32),
            jax.ShapeDtypeStruct((columns // 2, rows), BF16),
        ],
        scratch_shapes=[pltpu.VMEM((TILE, rows), F32)],
        compiler_params=pltpu.CompilerParams(vmem_limit_bytes=16 * 2**20),
        cost_estimate=pl.CostEstimate(
            flops=2 * rows * depth * columns,
            bytes_accessed=2 * depth * columns + 7 * rows * columns,
            transcendentals=0,
        ),
    )(core.reshape(1), x, w, more)


def exchange(x, axes):
    return lax.all_to_all(x, axes, split_axis=0, concat_axis=0, tiled=True)


def per_device(
    resid, query, new_kv, key_cache, value_cache, lengths, out_weight, hidden, down_weight
):
    high, low, core = lax.axis_index("gxh"), lax.axis_index("gxl"), lax.axis_index("core")
    gy = lax.axis_index(GY)

    cache = jnp.concatenate([key_cache, value_cache], -1).reshape(2, 2, 128, 2 * HD)
    other = lax.dynamic_index_in_dim(cache, 1 - low, 1, False).reshape(256, 2 * HD)
    own = jnp.pad(hidden.reshape(32, 288), ((0, 0), (0, 2 * HD - 288)))
    other = lax.ppermute(jnp.concatenate([other, own], 0), "gxl", [(0, 1), (1, 0)])
    near = other[256:, :288].reshape(2, 16, 288)
    other = other[:256].reshape(2, 128, 2 * HD)
    ours_of = lambda c: lax.dynamic_index_in_dim(c.reshape(2, 2, 128, HD), low, 1, False)
    keys = jnp.concatenate([ours_of(key_cache), other[..., :HD]], 1)
    values = jnp.concatenate([ours_of(value_cache), other[..., HD:]], 1)
    keys, near = lax.optimization_barrier((keys, near))
    near = jnp.where(low == 0, jnp.stack([hidden, near]), jnp.stack([near, hidden]))
    far = lax.ppermute(near, "gxh", [(0, 1), (1, 0)])

    pick = jnp.arange(64)
    pick = (pick // 2 % 2) * 64 + (pick // 4) * 4 + (pick % 2) * 2 + low
    pick = (pick[:, None] == jnp.arange(128)[None, :]).astype(BF16)
    q = jnp.dot(pick, query.reshape(128, 768), preferred_element_type=F32).astype(BF16)
    q = exchange(q.reshape(16, 4, 768), "gz")
    qf = q.reshape(16, 2, 2, 3, HD).transpose(2, 0, 1, 3, 4).reshape(2, 96, HD)

    at = jnp.arange(256, dtype=jnp.int32)
    owner = (high * 2 + jnp.where(at < 128, low, 1 - low)) * 8 + gy
    positions = owner * 128 + at % 128
    length = lax.dynamic_index_in_dim(lengths.reshape(2, 2), low, 1, False)
    fresh = lax.dynamic_index_in_dim(new_kv.reshape(2, 2, 2, 2 * HD), low, 2, False)
    present = (positions[None] < length[:, None])[:, None]
    scale = HD**-0.5
    s = jnp.einsum("bqd,bpd->bqp", qf, keys, preferred_element_type=F32) * scale
    s = jnp.where(present, s, NEG)
    step = (jnp.arange(96) // 3) % 2
    allowed = (jnp.arange(2)[None, :] <= step[:, None]) & (high + gy == 0)
    sn = jnp.einsum("bqd,ubd->bqu", qf, fresh[..., :HD], preferred_element_type=F32) * scale
    sn = jnp.where(allowed, sn, NEG)
    peak = jnp.maximum(jnp.max(s, -1), jnp.max(sn, -1)).astype(BF16)
    pf = peak.astype(F32)[..., None]
    w = jnp.where(present, jnp.exp(s - pf), 0.0).astype(BF16)
    wn = jnp.where(allowed, jnp.exp(sn - pf), 0.0).astype(BF16)
    total = jnp.sum(w.astype(F32), -1) + jnp.sum(wn.astype(F32), -1)
    acc = jnp.einsum("bqp,bpd->bqd", w, values, preferred_element_type=F32)
    acc = acc + jnp.einsum("bqu,ubd->bqd", wn, fresh[..., HD:], preferred_element_type=F32)
    total_hi = total.astype(BF16)
    total_lo = (total - total_hi.astype(F32)).astype(BF16)
    stats = jnp.stack([peak, total_hi, total_lo, jnp.zeros_like(peak)], 1)
    stats = stats.reshape(2, 4, 8, 12).transpose(0, 2, 1, 3).reshape(16, 4, 12)
    stats = jnp.pad(stats, ((0, 0), (0, 0), (0, HD - 12)))
    message = jnp.concatenate([acc.astype(BF16).reshape(16, 12, HD), stats], 1)

    message = exchange(message, ("gxh",) + GY)
    peaks = message[:, 12, :12].astype(F32)
    totals = message[:, 13, :12].astype(F32) + message[:, 14, :12].astype(F32)
    share = jnp.exp(peaks - jnp.max(peaks, 0))
    share = share / jnp.sum(share * totals, 0)
    attn = jnp.sum(message[:, :12].astype(F32) * share[..., None], 0).astype(BF16)
    attn = attn.reshape(2, 2, 3, HD).transpose(1, 0, 2, 3).reshape(2, 16, 96).transpose(1, 0, 2)
    attn = jnp.broadcast_to(attn[:, None], (16, 4, 2, 96)).reshape(64, 2, 96)

    spread = jnp.where(high == 0, jnp.concatenate([near, far]), jnp.concatenate([far, near]))
    feed = turned_product(spread.reshape(4, 32, 288), down_weight)

    mine = exchange(attn, ("gz",) + GX).transpose(1, 0, 2).reshape(128, 96)
    ours, theirs = split_product(core, mine, out_weight, feed)

    theirs = lax.ppermute(theirs, "core", [(0, 1), (1, 0)])
    row = (ours + theirs.astype(F32)).astype(BF16).reshape(4, 576, 128)
    row = exchange(row, "gyx")
    row = jnp.sum(row.astype(F32), 0).astype(BF16).reshape(16, 9, 4, 128)
    column = exchange(row, "gz").reshape(16, 36, 128)
    summed = jnp.sum(column.astype(F32), 0).reshape(36, 2, 64).transpose(1, 2, 0)
    return (summed + resid.astype(F32)).astype(BF16)


def solution(mesh):
    mesh = Mesh(mesh.devices.reshape(2, 2, 4, 2, 16), GX + GY + ("gz",))
    rows = GY + ("gz",)
    width = P(None, None, GX + rows)
    in_specs = (
        width,
        P(None, None, "gz"),
        P(None, "gz", None),
        P("gz", GX + GY, None),
        P("gz", GX + GY, None),
        P("gz"),
        P(rows, GX),
        P(None, GX, rows),
        P(rows, GX),
    )
    return jax.shard_map(
        per_device, mesh=mesh, in_specs=in_specs, out_specs=width, check_vma=False
    )
```

```python
import jax
import jax.numpy as jnp
from jax import lax
from jax.experimental import pallas as pl
from jax.experimental.pallas import tpu as pltpu
from jax.sharding import Mesh
from jax.sharding import PartitionSpec as P

HEADS = 48
HD = 256
F32 = jnp.float32
BF16 = jnp.bfloat16
GY = ("gyx", "core")
NEG = -1e30
TILE = 1152


def turned_product(gathered, w):
    shares, held, width = gathered.shape
    rows = shares * held
    columns = w.shape[1]
    tiles = columns // TILE

    def kernel(h_ref, w_hbm, o_ref, w_buf, sems):
        copies = []
        for i in range(tiles):
            place = pl.ds(i * TILE, TILE)
            copies.append(pltpu.make_async_copy(w_hbm.at[:, place], w_buf.at[i], sems.at[i]))
            copies[-1].start()
        hidden = jnp.concatenate(
            [h_ref[s, 16 * t : 16 * t + 16, :] for t in range(2) for s in range(shares)], 0
        )
        for i in range(tiles):
            copies[i].wait()
            y = jnp.dot(hidden, w_buf[i], preferred_element_type=F32)
            o_ref[pl.ds(i * TILE, TILE), :] = y.T

    in_vmem = pl.BlockSpec(memory_space=pltpu.VMEM)
    return pl.pallas_call(
        kernel,
        in_specs=[in_vmem, pl.BlockSpec(memory_space=pltpu.HBM)],
        out_specs=in_vmem,
        out_shape=jax.ShapeDtypeStruct((columns, rows), F32),
        scratch_shapes=[
            pltpu.VMEM((tiles, width, TILE), BF16),
            pltpu.SemaphoreType.DMA((tiles,)),
        ],
        compiler_params=pltpu.CompilerParams(vmem_limit_bytes=51 * 2**20),
        cost_estimate=pl.CostEstimate(
            flops=2 * rows * width * columns,
            bytes_accessed=2 * width * columns + 4 * rows * columns,
            transcendentals=0,
        ),
    )(gathered, w)


def split_product(core, x, w, more):
    rows, depth = x.shape
    columns = w.shape[1]
    half = TILE // 2

    def kernel(core_ref, x_ref, w_ref, more_ref, ours_ref, theirs_ref, full):
        mine = core_ref[0]
        for i in range(columns // TILE):
            place = pl.ds(i * TILE, TILE)
            y = jnp.dot(x_ref[...], w_ref[:, place], preferred_element_type=F32)
            full[...] = y.T + more_ref[place, :]
            rows_i = pl.ds(i * half, half)
            ours_ref[rows_i, :] = full[pl.ds(pl.multiple_of(mine * half, half), half), :]
            theirs = full[pl.ds(pl.multiple_of((1 - mine) * half, half), half), :]
            theirs_ref[rows_i, :] = theirs.astype(BF16)

    in_vmem = pl.BlockSpec(memory_space=pltpu.VMEM)
    return pl.pallas_call(
        kernel,
        in_specs=[pl.BlockSpec(memory_space=pltpu.SMEM), in_vmem, in_vmem, in_vmem],
        out_specs=[in_vmem, in_vmem],
        out_shape=[
            jax.ShapeDtypeStruct((columns // 2, rows), F32),
            jax.ShapeDtypeStruct((columns // 2, rows), BF16),
        ],
        scratch_shapes=[pltpu.VMEM((TILE, rows), F32)],
        compiler_params=pltpu.CompilerParams(vmem_limit_bytes=16 * 2**20),
        cost_estimate=pl.CostEstimate(
            flops=2 * rows * depth * columns,
            bytes_accessed=2 * depth * columns + 7 * rows * columns,
            transcendentals=0,
        ),
    )(core.reshape(1), x, w, more)


def exchange(x, axes):
    return lax.all_to_all(x, axes, split_axis=0, concat_axis=0, tiled=True)


def per_device(
    resid, query, new_kv, key_cache, value_cache, lengths, out_weight, hidden, down_weight
):
    gx, gyx, core = lax.axis_index("gx"), lax.axis_index("gyx"), lax.axis_index("core")

    pair = jnp.concatenate([key_cache, value_cache], -1)
    pair, own = lax.optimization_barrier((pair, hidden))
    pair = lax.ppermute(pair, "core", [(0, 1), (1, 0)])
    near = lax.ppermute(own, "gx", [(i, i ^ 1) for i in range(4)])
    keys = jnp.concatenate([key_cache, pair[..., :HD]], 1)
    values = jnp.concatenate([value_cache, pair[..., HD:]], 1)
    keys, near = lax.optimization_barrier((keys, near))
    near = jnp.where(gx % 2 == 0, jnp.stack([hidden, near]), jnp.stack([near, hidden]))
    far = lax.ppermute(near, "gx", [(i, i ^ 2) for i in range(4)])
    q = lax.dynamic_index_in_dim(query, core, 0, keepdims=False)
    q = exchange(q.reshape(16, 4, 768), "gz")
    qf = q.reshape(16, 4, 3, HD).transpose(1, 0, 2, 3).reshape(4, HEADS, HD)

    at = jnp.arange(256, dtype=jnp.int32)
    owner = gx * 8 + gyx * 2 + jnp.where(at < 128, core, 1 - core)
    positions = owner * 128 + at % 128
    present = (positions[None] < lengths[:, None])[:, None]
    scale = HD**-0.5
    s = jnp.einsum("bqd,bpd->bqp", qf, keys, preferred_element_type=F32) * scale
    s = jnp.where(present, s, NEG)
    allowed = ((jnp.arange(2) <= core) & (gx + gyx == 0))[None, None]
    sn = jnp.einsum("bqd,ubd->bqu", qf, new_kv[..., :HD], preferred_element_type=F32) * scale
    sn = jnp.where(allowed, sn, NEG)
    peak = jnp.maximum(jnp.max(s, -1), jnp.max(sn, -1)).astype(BF16)
    pf = peak.astype(F32)[..., None]
    w = jnp.where(present, jnp.exp(s - pf), 0.0).astype(BF16)
    wn = jnp.where(allowed, jnp.exp(sn - pf), 0.0).astype(BF16)
    total = jnp.sum(w.astype(F32), -1) + jnp.sum(wn.astype(F32), -1)
    acc = jnp.einsum("bqp,bpd->bqd", w, values, preferred_element_type=F32)
    acc = acc + jnp.einsum("bqu,ubd->bqd", wn, new_kv[..., HD:], preferred_element_type=F32)
    total_hi = total.astype(BF16)
    total_lo = (total - total_hi.astype(F32)).astype(BF16)
    stats = jnp.stack([peak, total_hi, total_lo, jnp.zeros_like(peak)], 1)
    stats = stats.reshape(4, 4, 4, 12).transpose(0, 2, 1, 3).reshape(16, 4, 12)
    stats = jnp.pad(stats, ((0, 0), (0, 0), (0, HD - 12)))
    message = jnp.concatenate([acc.astype(BF16).reshape(16, 12, HD), stats], 1)

    message = exchange(message, ("gx", "gyx"))
    peaks = message[:, 12, :12].astype(F32)
    totals = message[:, 13, :12].astype(F32) + message[:, 14, :12].astype(F32)
    share = jnp.exp(peaks - jnp.max(peaks, 0))
    share = share / jnp.sum(share * totals, 0)
    attn = jnp.sum(message[:, :12].astype(F32) * share[..., None], 0).astype(BF16)
    attn = jnp.broadcast_to(attn.reshape(1, 32, 96), (4, 32, 96)).reshape(128, 1, 96)

    spread = jnp.where(gx < 2, jnp.concatenate([near, far]), jnp.concatenate([far, near]))
    feed = turned_product(spread.reshape(4, 32, 288), down_weight)

    mine = exchange(attn, ("gx", "core", "gz"))
    mine = mine.reshape(4, 2, 16, 96).transpose(1, 2, 0, 3).reshape(128, 96)
    ours, theirs = split_product(core, mine, out_weight, feed)

    theirs = lax.ppermute(theirs, "core", [(0, 1), (1, 0)])
    row = (ours + theirs.astype(F32)).astype(BF16).reshape(4, 576, 128)
    row = exchange(row, "gyx")
    row = jnp.sum(row.astype(F32), 0).astype(BF16).reshape(16, 9, 4, 128)
    column = exchange(row, "gz").reshape(16, 36, 128)
    summed = jnp.sum(column.astype(F32), 0).reshape(36, 2, 64).transpose(1, 2, 0)
    return (summed + resid.astype(F32)).astype(BF16)


def solution(mesh):
    mesh = Mesh(mesh.devices.reshape(4, 4, 2, 16), ("gx", "gyx", "core", "gz"))
    rows = GY + ("gz",)
    width = P(None, None, ("gx",) + rows)
    in_specs = (
        width,
        P(None, None, "gz"),
        P(None, "gz", None),
        P("gz", ("gx",) + GY, None),
        P("gz", ("gx",) + GY, None),
        P("gz"),
        P(rows, "gx"),
        P(None, "gx", rows),
        P(rows, "gx"),
    )
    return jax.shard_map(
        per_device, mesh=mesh, in_specs=in_specs, out_specs=width, check_vma=False
    )
```

```python
import jax
import jax.numpy as jnp
from jax import lax
from jax.experimental import pallas as pl
from jax.experimental.pallas import tpu as pltpu
from jax.sharding import Mesh
from jax.sharding import PartitionSpec as P

HEADS = 48
HD = 256
F32 = jnp.float32
BF16 = jnp.bfloat16
GY = ("gyx", "core")
NEG = -1e30
TILE = 1152


def turned_product(gathered, w):
    shares, held, width = gathered.shape
    rows = shares * held
    columns = w.shape[1]
    tiles = columns // TILE

    def kernel(h_ref, w_hbm, o_ref, w_buf, sems):
        copies = []
        for i in range(tiles):
            place = pl.ds(i * TILE, TILE)
            copies.append(pltpu.make_async_copy(w_hbm.at[:, place], w_buf.at[i], sems.at[i]))
            copies[-1].start()
        hidden = jnp.concatenate(
            [h_ref[s, 16 * t : 16 * t + 16, :] for t in range(2) for s in range(shares)], 0
        )
        for i in range(tiles):
            copies[i].wait()
            y = jnp.dot(hidden, w_buf[i], preferred_element_type=F32)
            o_ref[pl.ds(i * TILE, TILE), :] = y.T

    in_vmem = pl.BlockSpec(memory_space=pltpu.VMEM)
    return pl.pallas_call(
        kernel,
        in_specs=[in_vmem, pl.BlockSpec(memory_space=pltpu.HBM)],
        out_specs=in_vmem,
        out_shape=jax.ShapeDtypeStruct((columns, rows), F32),
        scratch_shapes=[
            pltpu.VMEM((tiles, width, TILE), BF16),
            pltpu.SemaphoreType.DMA((tiles,)),
        ],
        compiler_params=pltpu.CompilerParams(vmem_limit_bytes=51 * 2**20),
        cost_estimate=pl.CostEstimate(
            flops=2 * rows * width * columns,
            bytes_accessed=2 * width * columns + 4 * rows * columns,
            transcendentals=0,
        ),
    )(gathered, w)


def split_product(core, x, w, more):
    rows, depth = x.shape
    columns = w.shape[1]
    half = TILE // 2

    def kernel(core_ref, x_ref, w_ref, more_ref, ours_ref, theirs_ref, full):
        mine = core_ref[0]
        for i in range(columns // TILE):
            place = pl.ds(i * TILE, TILE)
            y = jnp.dot(x_ref[...], w_ref[:, place], preferred_element_type=F32)
            full[...] = y.T + more_ref[place, :]
            rows_i = pl.ds(i * half, half)
            ours_ref[rows_i, :] = full[pl.ds(pl.multiple_of(mine * half, half), half), :]
            theirs = full[pl.ds(pl.multiple_of((1 - mine) * half, half), half), :]
            theirs_ref[rows_i, :] = theirs.astype(BF16)

    in_vmem = pl.BlockSpec(memory_space=pltpu.VMEM)
    return pl.pallas_call(
        kernel,
        in_specs=[pl.BlockSpec(memory_space=pltpu.SMEM), in_vmem, in_vmem, in_vmem],
        out_specs=[in_vmem, in_vmem],
        out_shape=[
            jax.ShapeDtypeStruct((columns // 2, rows), F32),
            jax.ShapeDtypeStruct((columns // 2, rows), BF16),
        ],
        scratch_shapes=[pltpu.VMEM((TILE, rows), F32)],
        compiler_params=pltpu.CompilerParams(vmem_limit_bytes=16 * 2**20),
        cost_estimate=pl.CostEstimate(
            flops=2 * rows * depth * columns,
            bytes_accessed=2 * depth * columns + 7 * rows * columns,
            transcendentals=0,
        ),
    )(core.reshape(1), x, w, more)


def exchange(x, axes):
    return lax.all_to_all(x, axes, split_axis=0, concat_axis=0, tiled=True)


def per_device(
    resid, query, new_kv, key_cache, value_cache, lengths, out_weight, hidden, down_weight
):
    gx, gyx, core = lax.axis_index("gx"), lax.axis_index("gyx"), lax.axis_index("core")

    pair = jnp.concatenate([key_cache, value_cache], -1)
    pair, own = lax.optimization_barrier((pair, hidden))
    pair = lax.ppermute(pair, "core", [(0, 1), (1, 0)])
    near = lax.ppermute(own, "gx", [(i, i ^ 1) for i in range(4)])
    fresh = jnp.pad(new_kv.transpose(1, 0, 2), ((0, 0), (0, 14), (0, 0)))
    keys = jnp.concatenate([key_cache, pair[..., :HD], fresh[..., :HD]], 1)
    values = jnp.concatenate([value_cache, pair[..., HD:], fresh[..., HD:]], 1)
    keys, near = lax.optimization_barrier((keys, near))
    near = jnp.where(gx % 2 == 0, jnp.stack([hidden, near]), jnp.stack([near, hidden]))
    far = lax.ppermute(near, "gx", [(i, i ^ 2) for i in range(4)])
    q = lax.dynamic_index_in_dim(query, core, 0, keepdims=False)
    q = exchange(q.reshape(16, 4, 768), "gz")
    qf = q.reshape(16, 4, 3, HD).transpose(1, 0, 2, 3).reshape(4, HEADS, HD)

    at = jnp.arange(272, dtype=jnp.int32)
    owner = gx * 8 + gyx * 2 + jnp.where(at < 128, core, 1 - core)
    positions = owner * 128 + at % 128
    allowed = (at - 256 <= core) & (gx + gyx == 0)
    present = jnp.where(at < 256, positions[None] < lengths[:, None], allowed[None])[:, None]
    s = jnp.einsum("bqd,bpd->bqp", qf, keys, preferred_element_type=F32) * HD**-0.5
    s = jnp.where(present, s, NEG)
    peak = jnp.max(s, -1).astype(BF16)
    w = jnp.where(present, jnp.exp(s - peak.astype(F32)[..., None]), 0.0).astype(BF16)
    total = jnp.sum(w.astype(F32), -1)
    acc = jnp.einsum("bqp,bpd->bqd", w, values, preferred_element_type=F32)
    total_hi = total.astype(BF16)
    total_lo = (total - total_hi.astype(F32)).astype(BF16)
    stats = jnp.stack([peak, total_hi, total_lo, jnp.zeros_like(peak)], 1)
    stats = stats.reshape(4, 4, 4, 12).transpose(0, 2, 1, 3).reshape(16, 4, 12)
    stats = jnp.pad(stats, ((0, 0), (0, 0), (0, HD - 12)))
    message = jnp.concatenate([acc.astype(BF16).reshape(16, 12, HD), stats], 1)

    message = exchange(message, ("gx", "gyx"))
    peaks = message[:, 12, :12].astype(F32)
    totals = message[:, 13, :12].astype(F32) + message[:, 14, :12].astype(F32)
    share = jnp.exp(peaks - jnp.max(peaks, 0))
    share = share / jnp.sum(share * totals, 0)
    attn = jnp.sum(message[:, :12].astype(F32) * share[..., None], 0).astype(BF16)
    attn = jnp.broadcast_to(attn.reshape(1, 32, 96), (4, 32, 96)).reshape(128, 1, 96)

    spread = jnp.where(gx < 2, jnp.concatenate([near, far]), jnp.concatenate([far, near]))
    feed = turned_product(spread.reshape(4, 32, 288), down_weight)

    mine = exchange(attn, ("gx", "core", "gz"))
    mine = mine.reshape(4, 2, 16, 96).transpose(1, 2, 0, 3).reshape(128, 96)
    ours, theirs = split_product(core, mine, out_weight, feed)

    theirs = lax.ppermute(theirs, "core", [(0, 1), (1, 0)])
    row = (ours + theirs.astype(F32)).astype(BF16).reshape(4, 576, 128)
    row = exchange(row, "gyx")
    row = jnp.sum(row.astype(F32), 0).astype(BF16).reshape(16, 9, 4, 128)
    column = exchange(row, "gz").reshape(16, 36, 128)
    summed = jnp.sum(column.astype(F32), 0).reshape(36, 2, 64).transpose(1, 2, 0)
    return (summed + resid.astype(F32)).astype(BF16)


def solution(mesh):
    mesh = Mesh(mesh.devices.reshape(4, 4, 2, 16), ("gx", "gyx", "core", "gz"))
    rows = GY + ("gz",)
    width = P(None, None, ("gx",) + rows)
    in_specs = (
        width,
        P(None, None, "gz"),
        P(None, "gz", None),
        P("gz", ("gx",) + GY, None),
        P("gz", ("gx",) + GY, None),
        P("gz"),
        P(rows, "gx"),
        P(None, "gx", rows),
        P(rows, "gx"),
    )
    return jax.shard_map(
        per_device, mesh=mesh, in_specs=in_specs, out_specs=width, check_vma=False
    )
```

```python
import jax
import jax.numpy as jnp
from jax import lax
from jax.experimental import pallas as pl
from jax.experimental.pallas import tpu as pltpu
from jax.sharding import Mesh
from jax.sharding import PartitionSpec as P

HEADS = 48
HD = 256
F32 = jnp.float32
BF16 = jnp.bfloat16
GY = ("gyx", "core")
NEG = -1e30
TILE = 1152


def turned_product(gathered, w):
    shares, held, width = gathered.shape
    rows = shares * held
    columns = w.shape[1]
    tiles = columns // TILE

    def kernel(h_ref, w_hbm, o_ref, w_buf, sems):
        copies = []
        for i in range(tiles):
            place = pl.ds(i * TILE, TILE)
            copies.append(pltpu.make_async_copy(w_hbm.at[:, place], w_buf.at[i], sems.at[i]))
            copies[-1].start()
        hidden = jnp.concatenate(
            [h_ref[s, 16 * t : 16 * t + 16, :] for t in range(2) for s in range(shares)], 0
        )
        for i in range(tiles):
            copies[i].wait()
            y = jnp.dot(hidden, w_buf[i], preferred_element_type=F32)
            o_ref[pl.ds(i * TILE, TILE), :] = y.T

    in_vmem = pl.BlockSpec(memory_space=pltpu.VMEM)
    return pl.pallas_call(
        kernel,
        in_specs=[in_vmem, pl.BlockSpec(memory_space=pltpu.HBM)],
        out_specs=in_vmem,
        out_shape=jax.ShapeDtypeStruct((columns, rows), F32),
        scratch_shapes=[
            pltpu.VMEM((tiles, width, TILE), BF16),
            pltpu.SemaphoreType.DMA((tiles,)),
        ],
        compiler_params=pltpu.CompilerParams(vmem_limit_bytes=51 * 2**20),
        cost_estimate=pl.CostEstimate(
            flops=2 * rows * width * columns,
            bytes_accessed=2 * width * columns + 4 * rows * columns,
            transcendentals=0,
        ),
    )(gathered, w)


def half_product(which, x, w, more, dtype):
    rows, depth = x.shape
    columns = w.shape[1]
    half = TILE // 2

    def kernel(which_ref, x_ref, w_ref, more_ref, o_ref, full):
        at = pl.multiple_of(which_ref[0] * half, half)
        for i in range(columns // TILE):
            y = jnp.dot(x_ref[...], w_ref[:, pl.ds(i * TILE, TILE)], preferred_element_type=F32)
            full[...] = y.T
            y = full[pl.ds(at, half), :] + more_ref[pl.ds(i * TILE + at, half), :]
            o_ref[pl.ds(i * half, half), :] = y.astype(dtype)

    in_vmem = pl.BlockSpec(memory_space=pltpu.VMEM)
    return pl.pallas_call(
        kernel,
        in_specs=[pl.BlockSpec(memory_space=pltpu.SMEM), in_vmem, in_vmem, in_vmem],
        out_specs=in_vmem,
        out_shape=jax.ShapeDtypeStruct((columns // 2, rows), dtype),
        scratch_shapes=[pltpu.VMEM((TILE, rows), F32)],
        compiler_params=pltpu.CompilerParams(vmem_limit_bytes=16 * 2**20),
        cost_estimate=pl.CostEstimate(
            flops=2 * rows * depth * columns,
            bytes_accessed=2 * depth * columns + 4 * rows * columns,
            transcendentals=0,
        ),
    )(which.reshape(1), x, w, more)


def exchange(x, axes):
    return lax.all_to_all(x, axes, split_axis=0, concat_axis=0, tiled=True)


def per_device(
    resid, query, new_kv, key_cache, value_cache, lengths, out_weight, hidden, down_weight
):
    gx, gyx, core = lax.axis_index("gx"), lax.axis_index("gyx"), lax.axis_index("core")

    pair = jnp.concatenate([key_cache, value_cache], -1)
    pair, own = lax.optimization_barrier((pair, hidden))
    pair = lax.ppermute(pair, "core", [(0, 1), (1, 0)])
    near = lax.ppermute(own, "gx", [(i, i ^ 1) for i in range(4)])
    keys = jnp.concatenate([key_cache, pair[..., :HD]], 1)
    values = jnp.concatenate([value_cache, pair[..., HD:]], 1)
    keys, near = lax.optimization_barrier((keys, near))
    near = jnp.where(gx % 2 == 0, jnp.stack([hidden, near]), jnp.stack([near, hidden]))
    far = lax.ppermute(near, "gx", [(i, i ^ 2) for i in range(4)])
    q = lax.dynamic_index_in_dim(query, core, 0, keepdims=False)
    q = exchange(q.reshape(16, 4, 768), "gz")
    qf = q.reshape(16, 4, 3, HD).transpose(1, 0, 2, 3).reshape(4, HEADS, HD)

    at = jnp.arange(256, dtype=jnp.int32)
    owner = gx * 8 + gyx * 2 + jnp.where(at < 128, core, 1 - core)
    positions = owner * 128 + at % 128
    present = (positions[None] < lengths[:, None])[:, None]
    scale = HD**-0.5
    s = jnp.einsum("bqd,bpd->bqp", qf, keys, preferred_element_type=F32) * scale
    s = jnp.where(present, s, NEG)
    allowed = ((jnp.arange(2) <= core) & (gx + gyx == 0))[None, None]
    sn = jnp.einsum("bqd,ubd->bqu", qf, new_kv[..., :HD], preferred_element_type=F32) * scale
    sn = jnp.where(allowed, sn, NEG)
    peak = jnp.maximum(jnp.max(s, -1), jnp.max(sn, -1)).astype(BF16)
    pf = peak.astype(F32)[..., None]
    w = jnp.where(present, jnp.exp(s - pf), 0.0).astype(BF16)
    wn = jnp.where(allowed, jnp.exp(sn - pf), 0.0).astype(BF16)
    total = jnp.sum(w.astype(F32), -1) + jnp.sum(wn.astype(F32), -1)
    acc = jnp.einsum("bqp,bpd->bqd", w, values, preferred_element_type=F32)
    acc = acc + jnp.einsum("bqu,ubd->bqd", wn, new_kv[..., HD:], preferred_element_type=F32)
    total_hi = total.astype(BF16)
    total_lo = (total - total_hi.astype(F32)).astype(BF16)
    stats = jnp.stack([peak, total_hi, total_lo, jnp.zeros_like(peak)], 1)
    stats = stats.reshape(4, 4, 4, 12).transpose(0, 2, 1, 3).reshape(16, 4, 12)
    stats = jnp.pad(stats, ((0, 0), (0, 0), (0, HD - 12)))
    message = jnp.concatenate([acc.astype(BF16).reshape(16, 12, HD), stats], 1)

    message = exchange(message, ("gx", "gyx"))
    peaks = message[:, 12, :12].astype(F32)
    totals = message[:, 13, :12].astype(F32) + message[:, 14, :12].astype(F32)
    share = jnp.exp(peaks - jnp.max(peaks, 0))
    share = share / jnp.sum(share * totals, 0)
    attn = jnp.sum(message[:, :12].astype(F32) * share[..., None], 0).astype(BF16)
    attn = jnp.broadcast_to(attn.reshape(1, 32, 96), (4, 32, 96)).reshape(128, 1, 96)

    spread = jnp.where(gx < 2, jnp.concatenate([near, far]), jnp.concatenate([far, near]))
    feed = turned_product(spread.reshape(4, 32, 288), down_weight)

    mine = exchange(attn, ("gx", "core", "gz"))
    mine = mine.reshape(4, 2, 16, 96).transpose(1, 2, 0, 3).reshape(128, 96)
    theirs = half_product(1 - core, mine, out_weight, feed, BF16)
    ours = half_product(core, mine, out_weight, feed, F32)

    theirs = lax.ppermute(theirs, "core", [(0, 1), (1, 0)])
    row = (ours + theirs.astype(F32)).astype(BF16).reshape(4, 576, 128)
    row = exchange(row, "gyx")
    row = jnp.sum(row.astype(F32), 0).astype(BF16).reshape(16, 9, 4, 128)
    column = exchange(row, "gz").reshape(16, 36, 128)
    summed = jnp.sum(column.astype(F32), 0).reshape(36, 2, 64).transpose(1, 2, 0)
    return (summed + resid.astype(F32)).astype(BF16)


def solution(mesh):
    mesh = Mesh(mesh.devices.reshape(4, 4, 2, 16), ("gx", "gyx", "core", "gz"))
    rows = GY + ("gz",)
    width = P(None, None, ("gx",) + rows)
    in_specs = (
        width,
        P(None, None, "gz"),
        P(None, "gz", None),
        P("gz", ("gx",) + GY, None),
        P("gz", ("gx",) + GY, None),
        P("gz"),
        P(rows, "gx"),
        P(None, "gx", rows),
        P(rows, "gx"),
    )
    return jax.shard_map(
        per_device, mesh=mesh, in_specs=in_specs, out_specs=width, check_vma=False
    )
```
